128 devices in a mesh: phi: 8 (over y, core), eta: 16 (over x, z).
Axes of the slice: x: 4, y: 4, z: 4, core: 2. Of those that a mesh axis runs over, the one named last changes fastest.
Arguments:
- edges: bfloat16 [262144, 128], P(('phi', 'eta')), may hold values from -6 to 6
- cotangent: bfloat16 [262144, 128], P(('phi', 'eta')), may hold values from -6 to 6
- send_rows: int32 [128, 128, 32], P(('phi', 'eta')), may hold values from 0 to 2047
- send_count: int32 [128, 128], P(('phi', 'eta')), may hold values from 1 to 32, as said below
- trip_local: int32 [1048576], P(('phi', 'eta')), may hold values from 0 to 2047
- trip_remote: int32 [1048576], P(('phi', 'eta')), may hold values from 0 to 4095, as said below
- w_first: bfloat16 [384, 256], replicated, may hold values from -0.3125 to 0.3125
- bias_first: float32 [256], replicated, may hold values from -4 to 4
- w_second: bfloat16 [256, 128], replicated, may hold values from -0.375 to 0.375
Outputs:
- new_edges: bfloat16 [262144, 128], P(('phi', 'eta'))
- edge_grad: bfloat16 [262144, 128], P(('phi', 'eta'))
- grad_first: float32 [384, 256], replicated
- grad_bias: float32 [256], replicated
- grad_second: float32 [256, 128], replicated
The draws below stay inside these ranges and needn't reach their ends.
Inputs may be any that keep to these rules, and one draw needn't show every extreme that they name: `send_count`: some destination device has every slot live from every source. `trip_remote`: each triplet names a live slot of a source device toward its own owner.
All inputs are finite; a program needn't handle non-finite values.
Results may differ from the reference program's by a relative error of at most 0.0053.
Values may be sent and summed in bfloat16 or wider, within the bound.
No kernel may reach another device: no remote copies, remote signals or barrier semaphores. Data moves between devices by JAX's collectives and lax.ppermute only.
A program may use at most 128 MiB of HBM per device.

```python
import jax
import jax.numpy as jnp
from jax import lax

F = 128
HID = 256
EDGE_DEV = 2048
TRIP_DEV = 8192
CAP = 32
NDEV = 128
IN = 384
EDGES = 262144
TRIPLETS = 1048576


def shared_counts(key):
    first = jax.random.fold_in(key, 7)
    second = jax.random.fold_in(key, 8)
    counts = jax.random.randint(first, (NDEV, NDEV), 1, CAP + 1)
    fullest = jax.random.randint(second, (), 0, NDEV)
    counts = jnp.where(jnp.arange(NDEV)[None, :] == fullest, CAP, counts)
    return (counts.astype(jnp.int32), fullest)


def draw_send_count(key, part):
    counts, fullest = shared_counts(key)
    return counts


def draw_trip_remote(key, part):
    counts, fullest = shared_counts(key)
    source = jax.random.randint(jax.random.fold_in(key, 11), (TRIPLETS,), 0, NDEV)
    spread = jax.random.randint(jax.random.fold_in(key, 12), (TRIPLETS,), 0, 1048576)
    position = jnp.arange(TRIPLETS)
    owner = position // TRIP_DEV
    live_count = counts[source, owner]
    slot = spread % live_count
    picked = source * CAP + slot
    picked = jnp.where(position == fullest * TRIP_DEV, 0, picked)
    picked = jnp.where(position == fullest * TRIP_DEV + TRIP_DEV - 1, NDEV * CAP - 1, picked)
    return picked.astype(jnp.int32)


def with_ends(drawn, rng, smallest, high):
    shape = drawn.shape
    index_at = [jax.random.randint(jax.random.fold_in(rng, axis), (), 0, shape[axis]) for axis in range(len(shape))]
    drawn = drawn.at[tuple(index_at)].set(smallest)
    longest = shape.index(max(shape))
    index_at[longest] = (index_at[longest] + 1) % shape[longest]
    return drawn.at[tuple(index_at)].set(high)


def block_scale(rng, extent, pieces, low, largest):
    def one(axis_at, parts):
        steps = jax.random.uniform(jax.random.fold_in(jax.random.fold_in(rng, 6), axis_at), (parts,), jnp.float32, low / len(pieces), largest / len(pieces))
        return jnp.repeat(jnp.exp(steps), extent[axis_at] // parts).reshape((-1,) + (1,) * (len(extent) - axis_at - 1))

    factor_of = one(*pieces[0])
    for cut in pieces[1:]:
        factor_of = factor_of * one(*cut)
    return factor_of


def scatter_about(rng, dims, scale, reach, split=(), kind=jnp.bfloat16):
    drawn = jax.random.normal(rng, dims, jnp.float32) * scale
    if len(split) > 0:
        drawn = block_scale(rng, dims, split, -0.22, 0.18) * drawn
    return jnp.clip(drawn, min=-reach, max=reach).astype(kind)


def setup_inputs(seed: int = 0) -> dict:
    keys = jax.random.split(jax.random.key(seed), 10)
    edges = scatter_about(keys[0], (EDGES, F), 1.0, 6.0, ((0, 128),))
    cotangent = scatter_about(keys[1], (EDGES, F), 1.0, 6.0, ((0, 128),))
    send_rows = with_ends(jax.random.randint(keys[2], (NDEV, NDEV, CAP), 0, EDGE_DEV), jax.random.fold_in(keys[2], 1), 0, EDGE_DEV - 1).astype(jnp.int32)
    send_count = draw_send_count(jax.random.fold_in(keys[9], 71), 0)
    trip_local = with_ends(jax.random.randint(keys[4], (TRIPLETS,), 0, EDGE_DEV), jax.random.fold_in(keys[4], 1), 0, EDGE_DEV - 1).astype(jnp.int32)
    trip_remote = draw_trip_remote(jax.random.fold_in(keys[9], 71), 0)
    w_first = scatter_about(keys[6], (IN, HID), IN ** -0.5, 0.3125)
    bias_first = scatter_about(keys[7], (HID,), 0.7, 4.0, (), jnp.float32)
    w_second = scatter_about(keys[8], (HID, F), HID ** -0.5, 0.375)
    return {"edges": edges, "cotangent": cotangent, "send_rows": send_rows, "send_count": send_count, "trip_local": trip_local, "trip_remote": trip_remote, "w_first": w_first, "bias_first": bias_first, "w_second": w_second}


def silu_slope(pre):
    sig = jax.nn.sigmoid(pre)
    return sig * (1.0 + pre * (1.0 - sig))


def owner_terms(owner, edges, cotangent, send_rows, send_count, trip_local, trip_remote, w_first, bias_first, w_second):
    rows = send_rows[:, owner, :]
    live = jnp.arange(CAP, dtype=jnp.int32)[None, :] < send_count[:, owner][:, None]
    global_rows = (jnp.arange(NDEV, dtype=jnp.int32)[:, None] * EDGE_DEV + rows).astype(jnp.int32)
    zero = jnp.zeros((), jnp.bfloat16)
    far_lat = jnp.where(live[:, :, None], edges[global_rows], zero).reshape(NDEV * CAP, F)
    far_cot = jnp.where(live[:, :, None], cotangent[global_rows], zero).reshape(NDEV * CAP, F)
    base = (owner * EDGE_DEV).astype(jnp.int32)
    own_lat = lax.dynamic_slice_in_dim(edges, base, EDGE_DEV, 0)
    own_cot = lax.dynamic_slice_in_dim(cotangent, base, EDGE_DEV, 0)
    tstart = (owner * TRIP_DEV).astype(jnp.int32)
    local_idx = lax.dynamic_slice_in_dim(trip_local, tstart, TRIP_DEV, 0)
    remote_idx = lax.dynamic_slice_in_dim(trip_remote, tstart, TRIP_DEV, 0)
    inner = own_lat[local_idx]
    inner_cot = own_cot[local_idx]
    outer = far_lat[remote_idx]
    outer_cot = far_cot[remote_idx]
    inner_f = inner.astype(jnp.float32)
    outer_f = outer.astype(jnp.float32)
    prod = (inner_f * outer_f).astype(jnp.bfloat16)
    joined = jnp.concatenate([inner, outer, prod], axis=1)
    pre = jnp.dot(joined, w_first, preferred_element_type=jnp.float32) + bias_first
    hidden = jax.nn.silu(pre).astype(jnp.bfloat16)
    message = jnp.dot(hidden, w_second, preferred_element_type=jnp.float32)
    local_msg = jax.ops.segment_sum(message, local_idx, EDGE_DEV)
    slot_msg = jax.ops.segment_sum(message, remote_idx, NDEV * CAP)
    dmsg = (inner_cot.astype(jnp.float32) + outer_cot.astype(jnp.float32)).astype(jnp.bfloat16)
    grad_second = jnp.dot(hidden.T, dmsg, preferred_element_type=jnp.float32)
    dpre = jnp.dot(dmsg, w_second.T, preferred_element_type=jnp.float32) * silu_slope(pre)
    dpre_b = dpre.astype(jnp.bfloat16)
    grad_first = jnp.dot(joined.T, dpre_b, preferred_element_type=jnp.float32)
    grad_bias = jnp.sum(dpre, axis=0)
    dx = jnp.dot(dpre_b, w_first.T, preferred_element_type=jnp.float32)
    d_inner = dx[:, :F] + dx[:, 2 * F:] * outer_f
    d_outer = dx[:, F:2 * F] + dx[:, 2 * F:] * inner_f
    local_grad = jax.ops.segment_sum(d_inner, local_idx, EDGE_DEV)
    slot_grad = jax.ops.segment_sum(d_outer, remote_idx, NDEV * CAP)
    slots = jnp.stack([slot_msg, slot_grad], axis=1).astype(jnp.bfloat16).reshape(NDEV, CAP, 2, F)
    slots = jnp.where(live[:, :, None, None], slots, zero)
    return base, global_rows, local_msg, local_grad, slots, grad_first, grad_bias, grad_second


def reference(edges, cotangent, send_rows, send_count, trip_local, trip_remote, w_first, bias_first, w_second):
    def step(carry, owner):
        msg_total, grad_total, acc_first, acc_bias, acc_second = carry
        base, global_rows, local_msg, local_grad, slots, g_first, g_bias, g_second = owner_terms(
            owner, edges, cotangent, send_rows, send_count, trip_local, trip_remote, w_first, bias_first, w_second)
        own_rows = base + jnp.arange(EDGE_DEV, dtype=jnp.int32)
        flat_rows = global_rows.reshape(-1)
        msg_total = msg_total.at[own_rows].add(local_msg)
        msg_total = msg_total.at[flat_rows].add(slots[:, :, 0, :].astype(jnp.float32).reshape(-1, F))
        grad_total = grad_total.at[own_rows].add(local_grad)
        grad_total = grad_total.at[flat_rows].add(slots[:, :, 1, :].astype(jnp.float32).reshape(-1, F))
        return (msg_total, grad_total, acc_first + g_first, acc_bias + g_bias, acc_second + g_second), None

    start = (jnp.zeros((EDGES, F), jnp.float32), jnp.zeros((EDGES, F), jnp.float32),
             jnp.zeros((IN, HID), jnp.float32), jnp.zeros((HID,), jnp.float32), jnp.zeros((HID, F), jnp.float32))
    final, _ = lax.scan(step, start, jnp.arange(NDEV, dtype=jnp.int32))
    msg_total, grad_total, grad_first, grad_bias, grad_second = final
    new_edges = (edges.astype(jnp.float32) + msg_total).astype(jnp.bfloat16)
    edge_grad = (cotangent.astype(jnp.float32) + grad_total).astype(jnp.bfloat16)
    return (new_edges, edge_grad, grad_first, grad_bias, grad_second)
```

```python
import functools

import jax
import jax.numpy as jnp
from jax import lax
from jax.experimental import pallas as pl
from jax.experimental.pallas import tpu as pltpu
from jax.sharding import PartitionSpec as P

AXES = ("phi", "eta")
BLOCK = 256
WINDOW = 256
BF16 = jnp.bfloat16
F32 = jnp.float32


def dot(a, b):
    return jnp.dot(a, b, preferred_element_type=F32)


def dot_rows(a, b):
    return lax.dot_general(a, b, (((0,), (0,)), ((), ())), preferred_element_type=F32)


def triplet_kernel(
    slots,
    base_ref,
    count_ref,
    col_ref,
    row_ref,
    own_ref,
    far_ref,
    w1_ref,
    w1t_ref,
    w2_ref,
    w2t_ref,
    bias_ref,
    inner_ref,
    slot_ref,
    grad_ref,
    gbias_ref,
    total_ref,
    part_ref,
):
    width = own_ref.shape[1] // 2
    step = pl.program_id(0)

    @pl.when(step == 0)
    def _():
        total_ref[...] = jnp.zeros_like(total_ref)
        grad_ref[...] = jnp.zeros_like(grad_ref)
        gbias_ref[...] = jnp.zeros_like(gbias_ref)

    base = base_ref[step]
    count = count_ref[step]

    def window(w):
        first = base + w * WINDOW
        return first, pl.multiple_of(jnp.minimum(first, slots - WINDOW), 16)

    def pick(w):
        first, start = window(w)
        col = col_ref[...]
        rel = jnp.where(col >= first, col - start, -1)
        lane = lax.broadcasted_iota(jnp.int32, rel.shape, 1)
        hot = jnp.concatenate(
            [(rel == lane + k * 128).astype(F32).astype(BF16) for k in range(WINDOW // 128)], axis=1
        )
        return dot(hot, far_ref[pl.ds(start, WINDOW), :])

    part_ref[...] = pick(0)

    @pl.when(count > 1)
    def _():
        def more(w, carry):
            part_ref[...] += pick(w)
            return carry

        lax.fori_loop(1, count, more, 0)

    far = part_ref[...]
    b = far[:, :width]
    gb = far[:, width:]
    own = own_ref[...]
    a = own[:, :width]
    ga = own[:, width:]
    af = a.astype(F32)
    prod = (af * b).astype(BF16)
    x = jnp.concatenate([a, b.astype(BF16), prod], axis=1)
    pre = dot(x, w1_ref[...]) + bias_ref[...]
    sig = jax.nn.sigmoid(pre)
    h = (pre * sig).astype(BF16)
    m = dot(h, w2_ref[...])
    dm = (ga.astype(F32) + gb).astype(BF16)
    dpre = dot(dm, w2t_ref[...]) * (sig * (1.0 + pre * (1.0 - sig)))
    dpre_b = dpre.astype(BF16)
    dx = dot(dpre_b, w1t_ref[...])
    dprod = dx[:, 2 * width :]
    da = dx[:, :width] + dprod * b
    db = dx[:, width : 2 * width] + dprod * af
    mb = m.astype(BF16)
    inner_ref[...] = jnp.concatenate([mb, da.astype(BF16)], axis=1)
    outer = jnp.concatenate([mb, db.astype(BF16)], axis=1)
    rows1 = x.shape[1]
    grad_ref[:rows1, :] += dot_rows(x, dpre_b)
    grad_ref[rows1:, :] += dot_rows(dm, h)
    gbias_ref[...] += jnp.sum(dpre, axis=0, keepdims=True)

    def put(w):
        first, start = window(w)
        row = row_ref[0]
        rel = jnp.where(row >= first, row - start, -1)
        at = lax.broadcasted_iota(jnp.int32, (WINDOW, row.shape[1]), 0)
        hot = (at == rel).astype(F32).astype(BF16)
        total_ref[pl.ds(start, WINDOW), :] += dot(hot, outer)

    put(0)

    @pl.when(count > 1)
    def _():
        def more(w, carry):
            put(w)
            return carry

        lax.fori_loop(1, count, more, 0)

    @pl.when(step == pl.num_programs(0) - 1)
    def _():
        slot_ref[...] = total_ref[...].astype(BF16)


def triplets(remote, own, far, w1, bias, w2):
    trips = remote.shape[0]
    slots, pair = far.shape
    width = pair // 2
    hid = w1.shape[1]
    rows1 = w1.shape[0]
    steps = trips // BLOCK
    blocks = remote.reshape(steps, BLOCK)
    base = jnp.minimum(blocks[:, 0] // 16 * 16, slots - WINDOW)
    count = (blocks[:, BLOCK - 1] - base) // WINDOW + 1
    col = jnp.broadcast_to(remote[:, None], (trips, 128))
    row = remote.reshape(steps, 1, BLOCK)

    def whole(shape):
        return pl.BlockSpec(shape, lambda i, *_: (0,) * len(shape), pipeline_mode=pl.Buffered(1))

    def blocked(cols):
        return pl.BlockSpec((BLOCK, cols), lambda i, *_: (i, 0))

    return pl.pallas_call(
        functools.partial(triplet_kernel, slots),
        grid_spec=pltpu.PrefetchScalarGridSpec(
            num_scalar_prefetch=2,
            grid=(steps,),
            in_specs=[
                blocked(128),
                pl.BlockSpec((1, 1, BLOCK), lambda i, *_: (i, 0, 0)),
                blocked(pair),
                whole((slots, pair)),
                whole((rows1, hid)),
                whole((hid, rows1)),
                whole((hid, width)),
                whole((width, hid)),
                whole((1, hid)),
            ],
            out_specs=[
                blocked(pair),
                whole((slots, pair)),
                whole((rows1 + width, hid)),
                whole((1, hid)),
            ],
            scratch_shapes=[
                pltpu.VMEM((slots, pair), F32),
                pltpu.VMEM((BLOCK, pair), F32),
            ],
        ),
        out_shape=[
            jax.ShapeDtypeStruct((trips, pair), BF16),
            jax.ShapeDtypeStruct((slots, pair), BF16),
            jax.ShapeDtypeStruct((rows1 + width, hid), F32),
            jax.ShapeDtypeStruct((1, hid), F32),
        ],
        compiler_params=pltpu.CompilerParams(
            dimension_semantics=("arbitrary",), vmem_limit_bytes=40 * 2**20
        ),
        cost_estimate=pl.CostEstimate(
            flops=2 * trips * 600000, bytes_accessed=20 * 2**20, transcendentals=trips * hid * 2
        ),
        name="triplets",
    )(base, count, col, row, own, far, w1, w1.T, w2, w2.T, bias[None, :])


def split(x):
    high = lax.reduce_precision(x, 8, 7)
    return high.astype(BF16), (x - high).astype(BF16)


def local(
    edges, cotangent, send_rows, send_count, trip_local, trip_remote, w_first, bias_first, w_second
):
    width = edges.shape[1]
    rows = edges.shape[0]
    ndev = lax.axis_size("phi") * lax.axis_size("eta")
    slots_per = send_rows.shape[2]
    slots = ndev * slots_per
    pair = 2 * width
    live = jnp.arange(slots_per, dtype=jnp.int32)[None, :] < send_count[0][:, None]
    chosen = jnp.where(live, send_rows[0], -1).reshape(slots)
    row_ids = jnp.arange(rows, dtype=jnp.int32)
    table = jnp.concatenate([edges, cotangent], axis=1)
    with jax.named_scope("pack"):
        hot = (chosen[:, None] == row_ids[None, :]).astype(BF16)
        outgoing = dot(hot, table).astype(BF16).reshape(ndev, slots_per, pair)
    arrived = lax.all_to_all(outgoing, AXES, split_axis=0, concat_axis=0, tiled=True)
    arrived = arrived.reshape(slots, pair)
    with jax.named_scope("order"):
        key = jnp.sort(trip_remote * rows + trip_local)
        remote = key // rows
        inner = key - remote * rows
    with jax.named_scope("own_rows"):
        own = dot((inner[:, None] == row_ids[None, :]).astype(BF16), table).astype(BF16)
    inner_sums, slot_sums, grads, gbias = triplets(
        remote, own, arrived, w_first, bias_first, w_second
    )
    hid = w_first.shape[1]
    per = grads.shape[0] // ndev
    high, low = split(grads)
    outbound = jnp.concatenate(
        [
            slot_sums.reshape(ndev, slots_per, pair),
            high.reshape(ndev, per, hid),
            low.reshape(ndev, per, hid),
        ],
        axis=1,
    )
    returned = lax.all_to_all(outbound, AXES, split_axis=0, concat_axis=0, tiled=True)
    with jax.named_scope("own_sums"):
        own_sum = dot((row_ids[:, None] == inner[None, :]).astype(BF16), inner_sums)
        own_sum = lax.optimization_barrier(table.astype(F32) + own_sum)
    mine = returned[:, slots_per:, :].astype(F32)
    mine = jnp.sum(mine[:, :per, :] + mine[:, per:, :], axis=0).astype(BF16)
    bias_high, bias_low = split(gbias)
    share = jnp.concatenate([mine, bias_high, bias_low, jnp.zeros((2, hid), BF16)], axis=0)
    share = jnp.broadcast_to(share[None], (ndev,) + share.shape)
    shared = lax.all_to_all(share, AXES, split_axis=0, concat_axis=0, tiled=True)
    with jax.named_scope("far_sums"):
        back = returned[:, :slots_per, :].reshape(slots, pair)
        far_sum = dot((row_ids[:, None] == chosen[None, :]).astype(BF16), back)
    both = (own_sum + far_sum).astype(BF16)
    total = shared[:, :per, :].reshape(ndev * per, hid).astype(F32)
    cut = w_first.shape[0]
    grad_bias = jnp.sum(shared[:, per : per + 2, :].astype(F32), axis=(0, 1))
    return (both[:, :width], both[:, width:], total[:cut], grad_bias, total[cut:].T)


def solution(mesh):
    in_specs = (
        P(AXES, None),
        P(AXES, None),
        P(AXES, None, None),
        P(AXES, None),
        P(AXES),
        P(AXES),
        P(),
        P(),
        P(),
    )
    out_specs = (P(AXES, None), P(AXES, None), P(), P(), P())
    return jax.shard_map(local, mesh=mesh, in_specs=in_specs, out_specs=out_specs, check_vma=False)
```

```python
import functools

import jax
import jax.numpy as jnp
from jax import lax
from jax.experimental import pallas as pl
from jax.experimental.pallas import tpu as pltpu
from jax.sharding import PartitionSpec as P

AXES = ("phi", "eta")
BLOCK = 2048
SUPER = 2048
CHUNK = 512
ORDER = (3, 2, 1, 0)
PART = 256
WINDOW = 256
BF16 = jnp.bfloat16
F32 = jnp.float32


def dot(a, b):
    return jnp.dot(a, b, preferred_element_type=F32)


def dot_rows(a, b):
    return lax.dot_general(a, b, (((0,), (0,)), ((), ())), preferred_element_type=F32)


def triplet_kernel(
    base_ref,
    count_ref,
    most_ref,
    row_ref,
    own_hbm,
    far_ref,
    w1_ref,
    w1t_ref,
    w2_ref,
    w2t_ref,
    bias_ref,
    inner_ref,
    out_ref,
    gbias_ref,
    total_ref,
    grad_ref,
    far2_ref,
    outer_ref,
    own_ref,
    own_sem,
):
    fetch = pltpu.make_async_copy(own_hbm, own_ref, own_sem)
    fetch.start()
    width = own_ref.shape[1] // 2
    slots = far_ref.shape[0]
    parts = BLOCK // PART
    ndev, _, pair = out_ref.shape
    slots_per = slots // ndev

    total_ref[...] = jnp.zeros_like(total_ref)
    grad_ref[...] = jnp.zeros_like(grad_ref)
    gbias_ref[...] = jnp.zeros_like(gbias_ref)

    def window(part, w):
        first = base_ref[part] + w * WINDOW
        start = pl.multiple_of(jnp.minimum(first, slots - WINDOW), 16)
        rel = row_ref[part] - start
        if not isinstance(w, int):
            rel = jnp.where(rel >= first - start, rel, -1)
        down = lax.broadcasted_iota(jnp.int32, (WINDOW, PART), 0)
        return pl.ds(start, WINDOW), (down == rel).astype(F32).astype(BF16)

    def place(part):
        return pl.ds(pl.multiple_of(part * PART, PART), PART)

    def gather(step, carry):
        for j in range(parts):
            part = step * parts + j
            span, hot = window(part, 0)
            far2_ref[place(part), :] = dot_rows(hot, far_ref[span, :]).astype(BF16)

        @pl.when(most_ref[step] > 1)
        def _():
            for j in range(parts):
                part = step * parts + j

                def more(w, carry):
                    span, hot = window(part, w)
                    far2_ref[place(part), :] += dot_rows(hot, far_ref[span, :]).astype(BF16)
                    return carry

                lax.fori_loop(1, count_ref[part], more, 0)

        return carry

    def mlp(step, carry):
        chunks = SUPER // CHUNK
        state = [dict() for _ in range(chunks)]

        def here(c):
            return pl.ds(pl.multiple_of(step * SUPER + c * CHUNK, CHUNK), CHUNK)

        def stage0(c):
            v = state[c]
            a = own_ref[here(c), :width]
            b = far2_ref[here(c), :width]
            prod = (a.astype(F32) * b.astype(F32)).astype(BF16)
            v["x"] = jnp.concatenate([a, b, prod], axis=1)
            v["pre"] = dot(v["x"], w1_ref[...]) + bias_ref[...]
            ga = own_ref[here(c), width:]
            gb = far2_ref[here(c), width:]
            v["dm"] = (ga.astype(F32) + gb.astype(F32)).astype(BF16)
            v["dh"] = dot(v["dm"], w2t_ref[...])

        def stage1(c):
            v = state[c]
            pre = v.pop("pre")
            sig = 0.5 * jnp.tanh(0.5 * pre) + 0.5
            v["h"] = (pre * sig).astype(BF16)
            dpre = v.pop("dh") * (sig * (1.0 + pre * (1.0 - sig)))
            gbias_ref[...] += jnp.sum(dpre, axis=0, keepdims=True)
            v["dpre"] = dpre.astype(BF16)

        def stage2(c):
            v = state[c]
            mb = dot(v["h"], w2_ref[...]).astype(BF16)
            inner_ref[here(c), :width] = mb
            outer_ref[here(c), :width] = mb
            v["dx"] = dot(v["dpre"], w1t_ref[...])

        def stage3(c):
            v = state[c]
            dx = v.pop("dx")
            af = own_ref[here(c), :width].astype(F32)
            b = far2_ref[here(c), :width].astype(F32)
            dprod = dx[:, 2 * width :]
            inner_ref[here(c), width:] = (dx[:, :width] + dprod * b).astype(BF16)
            outer_ref[here(c), width:] = (dx[:, width : 2 * width] + dprod * af).astype(BF16)
            rows1 = w1_ref.shape[0]
            grad_ref[:rows1, :] += dot_rows(v["x"], v["dpre"])
            grad_ref[rows1:, :] += dot_rows(v["dm"], v["h"])

        stages = [stage0, stage1, stage2, stage3]
        for t in range(chunks + len(stages) - 1):
            for s in ORDER:
                c = t - s
                if 0 <= c < chunks:
                    stages[s](c)
        return carry

    def scatter(step, carry):
        for j in range(parts):
            part = step * parts + j
            span, hot = window(part, 0)
            total_ref[span, :] += dot(hot, outer_ref[place(part), :])

        @pl.when(most_ref[step] > 1)
        def _():
            for j in range(parts):
                part = step * parts + j

                def more(w, carry):
                    span, hot = window(part, w)
                    total_ref[span, :] += dot(hot, outer_ref[place(part), :])
                    return carry

                lax.fori_loop(1, count_ref[part], more, 0)

        return carry

    trips = own_ref.shape[0]
    lax.fori_loop(0, trips // BLOCK, gather, 0)
    fetch.wait()
    lax.fori_loop(0, trips // SUPER, mlp, 0)
    lax.fori_loop(0, trips // BLOCK, scatter, 0)

    def close(d, carry):
        out_ref[d, :slots_per, :] = total_ref[
            pl.ds(pl.multiple_of(d * slots_per, slots_per), slots_per), :
        ].astype(BF16)
        return carry

    lax.fori_loop(0, ndev, close, 0, unroll=8)

    def close_grad(k, carry):
        for c in range(2):
            g = grad_ref[pl.ds(pl.multiple_of(k * 8, 8), 8), c * 128 : (c + 1) * 128]
            high = g.astype(BF16)
            low = (g - high.astype(F32)).astype(BF16)
            out_ref[2 * k + c, slots_per:, :] = jnp.concatenate([high, low], axis=1)
        return carry

    lax.fori_loop(0, ndev // 2, close_grad, 0, unroll=4)


def triplets(remote, own, far, w1, bias, w2, ndev):
    trips = remote.shape[0]
    slots, pair = far.shape
    width = pair // 2
    hid = w1.shape[1]
    rows1 = w1.shape[0]
    steps = trips // BLOCK
    parts = BLOCK // PART
    blocks = remote.reshape(steps * parts, PART)
    base = jnp.minimum(blocks[:, 0] // 16 * 16, slots - WINDOW)
    count = (blocks[:, PART - 1] - base) // WINDOW + 1
    most = jnp.max(count.reshape(steps, parts), axis=1)
    row = remote.reshape(steps * parts, 1, PART)
    smem = pl.BlockSpec(memory_space=pltpu.SMEM)
    vmem = pl.BlockSpec(memory_space=pltpu.VMEM)
    return pl.pallas_call(
        triplet_kernel,
        in_specs=[smem] * 3 + [vmem, pl.BlockSpec(memory_space=pl.ANY)] + [vmem] * 6,
        out_specs=[vmem] * 3,
        scratch_shapes=[
            pltpu.VMEM((slots, pair), F32),
            pltpu.VMEM((rows1 + width, hid), F32),
            pltpu.VMEM((trips, pair), BF16),
            pltpu.VMEM((trips, pair), BF16),
            pltpu.VMEM((trips, pair), BF16),
            pltpu.SemaphoreType.DMA,
        ],
        out_shape=[
            jax.ShapeDtypeStruct((trips, pair), BF16),
            jax.ShapeDtypeStruct((ndev, slots // ndev + 8, pair), BF16),
            jax.ShapeDtypeStruct((1, hid), F32),
        ],
        compiler_params=pltpu.CompilerParams(vmem_limit_bytes=36 * 2**20),
        cost_estimate=pl.CostEstimate(
            flops=2 * trips * 600000, bytes_accessed=20 * 2**20, transcendentals=trips * hid
        ),
        name="triplets",
    )(base, count, most, row, own, far, w1, w1.T, w2, w2.T, bias[None, :])


def split(x):
    high = lax.reduce_precision(x, 8, 7)
    return high.astype(BF16), (x - high).astype(BF16)


def local(
    edges, cotangent, send_rows, send_count, trip_local, trip_remote, w_first, bias_first, w_second
):
    width = edges.shape[1]
    rows = edges.shape[0]
    ndev = lax.axis_size("phi") * lax.axis_size("eta")
    slots_per = send_rows.shape[2]
    slots = ndev * slots_per
    pair = 2 * width
    live = jnp.arange(slots_per, dtype=jnp.int32)[None, :] < send_count[0][:, None]
    chosen = jnp.where(live, send_rows[0], -1).reshape(slots)
    row_ids = jnp.arange(rows, dtype=jnp.int32)
    table = jnp.concatenate([edges, cotangent], axis=1)
    with jax.named_scope("pack"):
        hot = (chosen[:, None] == row_ids[None, :]).astype(BF16)
        outgoing = dot(hot, table).astype(BF16).reshape(ndev, slots_per, pair)
    arrived = lax.all_to_all(outgoing, AXES, split_axis=0, concat_axis=0, tiled=True)
    arrived = arrived.reshape(slots, pair)
    with jax.named_scope("order"):
        key = jnp.sort(trip_remote * rows + trip_local)
        remote = key // rows
        inner = key - remote * rows
    with jax.named_scope("own_rows"):
        own = dot((inner[:, None] == row_ids[None, :]).astype(BF16), table).astype(BF16)
    inner_sums, outbound, gbias = triplets(
        remote, own, arrived, w_first, bias_first, w_second, ndev
    )
    returned = lax.all_to_all(outbound, AXES, split_axis=0, concat_axis=0, tiled=True)
    with jax.named_scope("own_sums"):
        own_sum = dot((row_ids[:, None] == inner[None, :]).astype(BF16), inner_sums)
        own_sum = lax.optimization_barrier(table.astype(F32) + own_sum)
    hid = w_first.shape[1]
    mine = jnp.sum(returned[:, slots_per:, :].astype(F32), axis=0)
    mine = (mine[:, :width] + mine[:, width:]).astype(BF16)
    bias_high, bias_low = split(gbias)
    ends = jnp.concatenate([bias_high, bias_low], axis=0).reshape(4, width)
    ends = jnp.pad(ends, ((0, 4), (0, 0)))
    share = jnp.concatenate([mine, ends], axis=1)
    share = jnp.broadcast_to(share[None], (ndev,) + share.shape)
    shared = lax.all_to_all(share, AXES, split_axis=0, concat_axis=0, tiled=True)
    with jax.named_scope("far_sums"):
        back = returned[:, :slots_per, :].reshape(slots, pair)
        far_sum = dot((row_ids[:, None] == chosen[None, :]).astype(BF16), back)
    both = (own_sum + far_sum).astype(BF16)
    total = shared[:, :, :width].astype(F32).reshape(ndev // 2, 2, 8, width)
    total = total.transpose(0, 2, 1, 3).reshape(ndev * 4, hid)
    cut = w_first.shape[0]
    grad_bias = jnp.sum(shared[:, :4, width:].astype(F32), axis=0).reshape(2, hid).sum(0)
    return (both[:, :width], both[:, width:], total[:cut], grad_bias, total[cut:].T)


def solution(mesh):
    in_specs = (
        P(AXES, None),
        P(AXES, None),
        P(AXES, None, None),
        P(AXES, None),
        P(AXES),
        P(AXES),
        P(),
        P(),
        P(),
    )
    out_specs = (P(AXES, None), P(AXES, None), P(), P(), P())
    return jax.shard_map(local, mesh=mesh, in_specs=in_specs, out_specs=out_specs, check_vma=False)
```

```python
import functools

import jax
import jax.numpy as jnp
from jax import lax
from jax.experimental import pallas as pl
from jax.experimental.pallas import tpu as pltpu
from jax.sharding import PartitionSpec as P

AXES = ("phi", "eta")
BLOCK = 2048
PACK = 1024
SUPER = 2048
CHUNK = 512
ORDER = (3, 2, 1, 0)
PART = 256
WINDOW = 256
BF16 = jnp.bfloat16
F32 = jnp.float32


def dot(a, b):
    return jnp.dot(a, b, preferred_element_type=F32)


def dot_rows(a, b):
    return lax.dot_general(a, b, (((0,), (0,)), ((), ())), preferred_element_type=F32)


def triplet_kernel(
    base_ref,
    count_ref,
    most_ref,
    row_ref,
    own_hbm,
    far_ref,
    w1_ref,
    w1t_ref,
    w2_ref,
    w2t_ref,
    bias_ref,
    inner_hbm,
    dpre_hbm,
    out_ref,
    gbias_ref,
    total_ref,
    grad_ref,
    far2_ref,
    outer_ref,
    own_ref,
    inner_ref,
    dpre_ref,
    own_sem,
    keep_sem,
):
    fetch = pltpu.make_async_copy(own_hbm, own_ref, own_sem)
    fetch.start()
    width = own_ref.shape[1] // 2
    slots = far_ref.shape[0]
    parts = BLOCK // PART
    ndev, _, pair = out_ref.shape
    slots_per = slots // ndev

    total_ref[...] = jnp.zeros_like(total_ref)
    grad_ref[...] = jnp.zeros_like(grad_ref)
    gbias_ref[...] = jnp.zeros_like(gbias_ref)

    def window(part, w):
        first = base_ref[part] + w * WINDOW
        start = pl.multiple_of(jnp.minimum(first, slots - WINDOW), 16)
        rel = row_ref[part] - start
        if not isinstance(w, int):
            rel = jnp.where(rel >= first - start, rel, -1)
        down = lax.broadcasted_iota(jnp.int32, (WINDOW, PART), 0)
        return pl.ds(start, WINDOW), (down == rel).astype(F32).astype(BF16)

    def place(part):
        return pl.ds(pl.multiple_of(part * PART, PART), PART)

    def gather(step, carry):
        for j in range(parts):
            part = step * parts + j
            span, hot = window(part, 0)
            far2_ref[place(part), :] = dot_rows(hot, far_ref[span, :]).astype(BF16)

        @pl.when(most_ref[step] > 1)
        def _():
            for j in range(parts):
                part = step * parts + j

                def more(w, carry):
                    span, hot = window(part, w)
                    far2_ref[place(part), :] += dot_rows(hot, far_ref[span, :]).astype(BF16)
                    return carry

                lax.fori_loop(1, count_ref[part], more, 0)

        return carry

    def keeps(step):
        rows = pl.ds(pl.multiple_of(step * SUPER, SUPER), SUPER)
        return (
            pltpu.make_async_copy(inner_ref.at[rows], inner_hbm.at[rows], keep_sem.at[0, step]),
            pltpu.make_async_copy(dpre_ref.at[rows], dpre_hbm.at[rows], keep_sem.at[1, step]),
        )

    def mlp(step, carry):
        chunks = SUPER // CHUNK
        state = [dict() for _ in range(chunks)]

        def here(c):
            return pl.ds(pl.multiple_of(step * SUPER + c * CHUNK, CHUNK), CHUNK)

        def stage0(c):
            v = state[c]
            a = own_ref[here(c), :width]
            b = far2_ref[here(c), :width]
            prod = (a.astype(F32) * b.astype(F32)).astype(BF16)
            v["x"] = jnp.concatenate([a, b, prod], axis=1)
            v["pre"] = dot(v["x"], w1_ref[...]) + bias_ref[...]
            ga = own_ref[here(c), width:]
            gb = far2_ref[here(c), width:]
            v["dm"] = (ga.astype(F32) + gb.astype(F32)).astype(BF16)
            v["dh"] = dot(v["dm"], w2t_ref[...])

        def stage1(c):
            v = state[c]
            pre = v.pop("pre")
            sig = 0.5 * jnp.tanh(0.5 * pre) + 0.5
            v["h"] = (pre * sig).astype(BF16)
            dpre = v.pop("dh") * (sig * (1.0 + pre * (1.0 - sig)))
            gbias_ref[...] += jnp.sum(dpre, axis=0, keepdims=True)
            v["dpre"] = dpre.astype(BF16)
            dpre_ref[here(c), :] = v["dpre"]

        def stage2(c):
            v = state[c]
            mb = dot(v["h"], w2_ref[...]).astype(BF16)
            inner_ref[here(c), :width] = mb
            outer_ref[here(c), :width] = mb
            v["dx"] = dot(v["dpre"], w1t_ref[...])

        def stage3(c):
            v = state[c]
            dx = v.pop("dx")
            af = own_ref[here(c), :width].astype(F32)
            b = far2_ref[here(c), :width].astype(F32)
            dprod = dx[:, width:]
            inner_ref[here(c), width:] = (dprod * b).astype(BF16)
            outer_ref[here(c), width:] = (dx[:, :width] + dprod * af).astype(BF16)
            rows1 = w1_ref.shape[0]
            grad_ref[:rows1, :] += dot_rows(v["x"], v["dpre"])
            grad_ref[rows1:, :] += dot_rows(v["dm"], v["h"])

        stages = [stage0, stage1, stage2, stage3]
        for t in range(chunks + len(stages) - 1):
            for s in ORDER:
                c = t - s
                if 0 <= c < chunks:
                    stages[s](c)
        for copy in keeps(step):
            copy.start()
        return carry

    def scatter(step, carry):
        for j in range(parts):
            part = step * parts + j
            span, hot = window(part, 0)
            total_ref[span, :] += dot(hot, outer_ref[place(part), :])

        @pl.when(most_ref[step] > 1)
        def _():
            for j in range(parts):
                part = step * parts + j

                def more(w, carry):
                    span, hot = window(part, w)
                    total_ref[span, :] += dot(hot, outer_ref[place(part), :])
                    return carry

                lax.fori_loop(1, count_ref[part], more, 0)

        return carry

    trips = own_ref.shape[0]
    lax.fori_loop(0, trips // BLOCK, gather, 0)
    fetch.wait()
    lax.fori_loop(0, trips // SUPER, mlp, 0)
    lax.fori_loop(0, trips // BLOCK, scatter, 0)

    def close(d, carry):
        out_ref[d, :slots_per, :] = total_ref[
            pl.ds(pl.multiple_of(d * slots_per, slots_per), slots_per), :
        ].astype(BF16)
        return carry

    lax.fori_loop(0, ndev, close, 0, unroll=8)

    def close_grad(k, carry):
        for c in range(2):
            g = grad_ref[pl.ds(pl.multiple_of(k * 8, 8), 8), c * 128 : (c + 1) * 128]
            high = g.astype(BF16)
            low = (g - high.astype(F32)).astype(BF16)
            out_ref[2 * k + c, slots_per:, :] = jnp.concatenate([high, low], axis=1)
        return carry

    lax.fori_loop(0, ndev // 2, close_grad, 0, unroll=4)

    for step in range(trips // SUPER):
        for copy in keeps(step):
            copy.wait()


def triplets(remote, own, far, w1, bias, w2, ndev):
    trips = remote.shape[0]
    slots, pair = far.shape
    width = pair // 2
    hid = w1.shape[1]
    rows1 = w1.shape[0]
    steps = trips // BLOCK
    parts = BLOCK // PART
    blocks = remote.reshape(steps * parts, PART)
    base = jnp.minimum(blocks[:, 0] // 16 * 16, slots - WINDOW)
    count = (blocks[:, PART - 1] - base) // WINDOW + 1
    most = jnp.max(count.reshape(steps, parts), axis=1)
    row = remote.reshape(steps * parts, 1, PART)
    smem = pl.BlockSpec(memory_space=pltpu.SMEM)
    vmem = pl.BlockSpec(memory_space=pltpu.VMEM)
    hbm = pl.BlockSpec(memory_space=pltpu.HBM)
    return pl.pallas_call(
        triplet_kernel,
        in_specs=[smem] * 3 + [vmem, hbm] + [vmem] * 6,
        out_specs=[hbm, hbm, vmem, vmem],
        scratch_shapes=[
            pltpu.VMEM((slots, pair), F32),
            pltpu.VMEM((rows1 + width, hid), F32),
            pltpu.VMEM((trips, pair), BF16),
            pltpu.VMEM((trips, pair), BF16),
            pltpu.VMEM((trips, pair), BF16),
            pltpu.VMEM((trips, pair), BF16),
            pltpu.VMEM((trips, hid), BF16),
            pltpu.SemaphoreType.DMA,
            pltpu.SemaphoreType.DMA((2, trips // SUPER)),
        ],
        out_shape=[
            pltpu.HBM((trips, pair), BF16),
            pltpu.HBM((trips, hid), BF16),
            jax.ShapeDtypeStruct((ndev, slots // ndev + 8, pair), BF16),
            jax.ShapeDtypeStruct((1, hid), F32),
        ],
        compiler_params=pltpu.CompilerParams(vmem_limit_bytes=36 * 2**20),
        cost_estimate=pl.CostEstimate(
            flops=2 * trips * 600000, bytes_accessed=20 * 2**20, transcendentals=trips * hid
        ),
        name="triplets",
    )(base, count, most, row, pltpu.with_memory_space_constraint(own, pltpu.HBM), far, w1, w1[width:].T, w2, w2.T, bias[None, :])


def pack_kernel(
    edges_ref,
    cot_ref,
    rows_ref,
    count_ref,
    table_hbm,
    out_hbm,
    table_ref,
    index_ref,
    out_ref,
    table_sem,
    out_sem,
):
    rows, width = edges_ref.shape
    slots_per, ndev = rows_ref.shape
    block = out_ref.shape[1]
    group = block // slots_per
    table_ref[:, :width] = edges_ref[...]
    table_ref[:, width:] = cot_ref[...]
    keep = pltpu.make_async_copy(table_ref, table_hbm, table_sem)
    keep.start()
    slot = lax.broadcasted_iota(jnp.int32, (slots_per, ndev), 0)
    chosen = jnp.where(slot < count_ref[...], rows_ref[...], -1)
    for d in range(ndev):
        index_ref[d // group, (d % group) * slots_per : (d % group + 1) * slots_per, :] = (
            jnp.broadcast_to(chosen[:, d : d + 1], (slots_per, 128))
        )

    def send(g):
        start = pl.multiple_of(g * block, block)
        return pltpu.make_async_copy(out_ref.at[g], out_hbm.at[pl.ds(start, block)], out_sem.at[g])

    def body(g, carry):
        index = index_ref[g]
        lane = lax.broadcasted_iota(jnp.int32, index.shape, 1)
        hot = jnp.concatenate(
            [(index == lane + k * 128).astype(F32).astype(BF16) for k in range(rows // 128)], axis=1
        )
        out_ref[g] = dot(hot, table_ref[...]).astype(BF16)
        send(g).start()
        return carry

    groups = out_ref.shape[0]
    lax.fori_loop(0, groups, body, 0)
    for g in range(groups):
        send(g).wait()
    keep.wait()


def pack(edges, cotangent, rows_t, count):
    rows, width = edges.shape
    slots_per, ndev = rows_t.shape
    slots = slots_per * ndev
    groups = slots // PACK
    vmem = pl.BlockSpec(memory_space=pltpu.VMEM)
    return pl.pallas_call(
        pack_kernel,
        in_specs=[vmem] * 4,
        out_specs=[pl.BlockSpec(memory_space=pltpu.HBM)] * 2,
        out_shape=[
            pltpu.HBM((rows, 2 * width), BF16),
            pltpu.HBM((slots, 2 * width), BF16),
        ],
        scratch_shapes=[
            pltpu.VMEM((rows, 2 * width), BF16),
            pltpu.VMEM((groups, PACK, 128), jnp.int32),
            pltpu.VMEM((groups, PACK, 2 * width), BF16),
            pltpu.SemaphoreType.DMA,
            pltpu.SemaphoreType.DMA((groups,)),
        ],
        compiler_params=pltpu.CompilerParams(vmem_limit_bytes=36 * 2**20),
        cost_estimate=pl.CostEstimate(
            flops=4 * slots * rows * width, bytes_accessed=4 * 2**20, transcendentals=0
        ),
        name="pack",
    )(edges, cotangent, rows_t, count)


def unpack_kernel(shared_ref, first_ref, bias_ref, second_ref):
    width = shared_ref.shape[2] // 2
    cut = first_ref.shape[0] // 8
    for k in range(cut):
        for c in range(2):
            first_ref[8 * k : 8 * k + 8, c * width : (c + 1) * width] = shared_ref[
                2 * k + c, :, :width
            ].astype(F32)
    rest = shared_ref.shape[0] // 2 - cut
    for c in range(2):
        tall = jnp.concatenate(
            [shared_ref[2 * (cut + k) + c, :, :width].astype(F32) for k in range(rest)], axis=0
        )
        second_ref[c * width : (c + 1) * width, :] = tall.T
    ends = jnp.sum(shared_ref[:, :, width:].astype(F32), axis=0)
    for c in range(2):
        bias_ref[:, c * width : (c + 1) * width] = ends[c : c + 1, :] + ends[c + 2 : c + 3, :]


def unpack(shared, rows1, hid, width):
    vmem = pl.BlockSpec(memory_space=pltpu.VMEM)
    return pl.pallas_call(
        unpack_kernel,
        in_specs=[vmem],
        out_specs=[vmem] * 3,
        out_shape=[
            jax.ShapeDtypeStruct((rows1, hid), F32),
            jax.ShapeDtypeStruct((1, hid), F32),
            jax.ShapeDtypeStruct((hid, width), F32),
        ],
        cost_estimate=pl.CostEstimate(flops=0, bytes_accessed=2**20, transcendentals=0),
        name="unpack",
    )(pltpu.with_memory_space_constraint(shared, pltpu.VMEM))


def split(x):
    high = lax.reduce_precision(x, 8, 7)
    return high.astype(BF16), (x - high).astype(BF16)


def local(
    edges, cotangent, send_rows, send_count, trip_local, trip_remote, w_first, bias_first, w_second
):
    width = edges.shape[1]
    rows = edges.shape[0]
    ndev = lax.axis_size("phi") * lax.axis_size("eta")
    slots_per = send_rows.shape[2]
    slots = ndev * slots_per
    pair = 2 * width
    live = jnp.arange(slots_per, dtype=jnp.int32)[None, :] < send_count[0][:, None]
    chosen = jnp.where(live, send_rows[0], -1).reshape(slots)
    row_ids = jnp.arange(rows, dtype=jnp.int32)
    table, outgoing = pack(edges, cotangent, send_rows[0].T, send_count)
    outgoing = outgoing.reshape(ndev, slots_per, pair)
    arrived = lax.all_to_all(outgoing, AXES, split_axis=0, concat_axis=0, tiled=True)
    arrived = arrived.reshape(slots, pair)
    with jax.named_scope("order"):
        key = jnp.sort(trip_remote * rows + trip_local)
        remote = key // rows
        inner = key - remote * rows
    with jax.named_scope("own_rows"):
        own = dot((inner[:, None] == row_ids[None, :]).astype(BF16), table).astype(BF16)
    kept, dpre, outbound, gbias = triplets(
        remote, own, arrived, w_first, bias_first, w_second, ndev
    )
    returned = lax.all_to_all(outbound, AXES, split_axis=0, concat_axis=0, tiled=True)
    with jax.named_scope("own_sums"):
        d_inner = dot(dpre, w_first[:width].T) + kept[:, width:].astype(F32)
        inner_sums = jnp.concatenate([kept[:, :width], d_inner.astype(BF16)], axis=1)
        own_sum = dot((row_ids[:, None] == inner[None, :]).astype(BF16), inner_sums)
        own_sum = lax.optimization_barrier(table.astype(F32) + own_sum)
    hid = w_first.shape[1]
    mine = jnp.sum(returned[:, slots_per:, :].astype(F32), axis=0)
    mine = (mine[:, :width] + mine[:, width:]).astype(BF16)
    bias_high, bias_low = split(gbias)
    ends = jnp.concatenate([bias_high, bias_low], axis=0).reshape(4, width)
    ends = jnp.pad(ends, ((0, 4), (0, 0)))
    share = jnp.concatenate([mine, ends], axis=1)
    share = jnp.broadcast_to(share[None], (ndev,) + share.shape)
    shared = lax.all_to_all(share, AXES, split_axis=0, concat_axis=0, tiled=True)
    with jax.named_scope("far_sums"):
        back = returned[:, :slots_per, :].reshape(slots, pair)
        far_sum = dot((row_ids[:, None] == chosen[None, :]).astype(BF16), back)
    both = (own_sum + far_sum).astype(BF16)
    grad_first, grad_bias, grad_second = unpack(shared, w_first.shape[0], hid, width)
    return (both[:, :width], both[:, width:], grad_first, grad_bias.reshape(hid), grad_second)


def solution(mesh):
    in_specs = (
        P(AXES, None),
        P(AXES, None),
        P(AXES, None, None),
        P(AXES, None),
        P(AXES),
        P(AXES),
        P(),
        P(),
        P(),
    )
    out_specs = (P(AXES, None), P(AXES, None), P(), P(), P())
    return jax.shard_map(local, mesh=mesh, in_specs=in_specs, out_specs=out_specs, check_vma=False)
```

```python
import functools

import jax
import jax.numpy as jnp
from jax import lax
from jax.experimental import pallas as pl
from jax.experimental.pallas import tpu as pltpu
from jax.sharding import PartitionSpec as P

AXES = ("phi", "eta")
BLOCK = 2048
GROUP = 16
PACK = 1024
SUPER = 4096
CHUNK = 512
ORDER = (3, 2, 1, 0)
PART = 256
WINDOW = 256
BF16 = jnp.bfloat16
F32 = jnp.float32


def dot(a, b):
    return jnp.dot(a, b, preferred_element_type=F32)


def dot_rows(a, b):
    return lax.dot_general(a, b, (((0,), (0,)), ((), ())), preferred_element_type=F32)


def triplet_kernel(
    base_ref,
    count_ref,
    most_ref,
    row_ref,
    own_hbm,
    far_ref,
    w1_ref,
    w1t_ref,
    w2_ref,
    w2t_ref,
    bias_ref,
    inner_hbm,
    dpre_hbm,
    out_hbm,
    gbias_ref,
    total_ref,
    grad_ref,
    far2_ref,
    outer_ref,
    own_ref,
    inner_ref,
    dpre_ref,
    out_ref,
    own_sem,
    keep_sem,
    out_sem,
):
    trips = own_ref.shape[0]

    def fetch(step):
        rows = pl.ds(pl.multiple_of(step * SUPER, SUPER), SUPER)
        return pltpu.make_async_copy(own_hbm.at[rows], own_ref.at[rows], own_sem.at[step])

    for step in range(trips // SUPER):
        fetch(step).start()
    width = own_ref.shape[1] // 2
    slots = far_ref.shape[0]
    parts = BLOCK // PART
    ndev = out_ref.shape[0]
    slots_per = slots // ndev

    total_ref[...] = jnp.zeros_like(total_ref)
    grad_ref[...] = jnp.zeros_like(grad_ref)
    gbias_ref[...] = jnp.zeros_like(gbias_ref)

    def window(part, w):
        first = base_ref[part] + w * WINDOW
        start = pl.multiple_of(jnp.minimum(first, slots - WINDOW), 16)
        rel = row_ref[part] - start
        if not isinstance(w, int):
            rel = jnp.where(rel >= first - start, rel, -1)
        down = lax.broadcasted_iota(jnp.int32, (WINDOW, PART), 0)
        return pl.ds(start, WINDOW), (down == rel).astype(F32).astype(BF16)

    def place(part):
        return pl.ds(pl.multiple_of(part * PART, PART), PART)

    def gather(step, carry):
        for j in range(parts):
            part = step * parts + j
            span, hot = window(part, 0)
            far2_ref[place(part), :] = dot_rows(hot, far_ref[span, :]).astype(BF16)

        @pl.when(most_ref[step] > 1)
        def _():
            for j in range(parts):
                part = step * parts + j

                def more(w, carry):
                    span, hot = window(part, w)
                    far2_ref[place(part), :] += dot_rows(hot, far_ref[span, :]).astype(BF16)
                    return carry

                lax.fori_loop(1, count_ref[part], more, 0)

        return carry

    def keeps(step):
        rows = pl.ds(pl.multiple_of(step * SUPER, SUPER), SUPER)
        return (
            pltpu.make_async_copy(inner_ref.at[rows], inner_hbm.at[rows], keep_sem.at[0, step]),
            pltpu.make_async_copy(dpre_ref.at[rows], dpre_hbm.at[rows], keep_sem.at[1, step]),
        )

    def mlp(step, carry):
        fetch(step).wait()
        chunks = SUPER // CHUNK
        state = [dict() for _ in range(chunks)]

        def here(c):
            return pl.ds(pl.multiple_of(step * SUPER + c * CHUNK, CHUNK), CHUNK)

        def stage0(c):
            v = state[c]
            a = own_ref[here(c), :width]
            b = far2_ref[here(c), :width]
            prod = (a.astype(F32) * b.astype(F32)).astype(BF16)
            v["x"] = jnp.concatenate([a, b, prod], axis=1)
            v["pre"] = dot(v["x"], w1_ref[...]) + bias_ref[...]
            ga = own_ref[here(c), width:]
            gb = far2_ref[here(c), width:]
            v["dm"] = (ga.astype(F32) + gb.astype(F32)).astype(BF16)
            v["dh"] = dot(v["dm"], w2t_ref[...])

        def stage1(c):
            v = state[c]
            pre = v.pop("pre")
            sig = 0.5 * jnp.tanh(0.5 * pre) + 0.5
            v["h"] = (pre * sig).astype(BF16)
            dpre = v.pop("dh") * (sig * (1.0 + pre * (1.0 - sig)))
            gbias_ref[...] += jnp.sum(dpre, axis=0, keepdims=True)
            v["dpre"] = dpre.astype(BF16)
            dpre_ref[here(c), :] = v["dpre"]

        def stage2(c):
            v = state[c]
            mb = dot(v["h"], w2_ref[...]).astype(BF16)
            inner_ref[here(c), :width] = mb
            outer_ref[here(c), :width] = mb
            v["dx"] = dot(v["dpre"], w1t_ref[...])

        def stage3(c):
            v = state[c]
            dx = v.pop("dx")
            af = own_ref[here(c), :width].astype(F32)
            b = far2_ref[here(c), :width].astype(F32)
            dprod = dx[:, width:]
            inner_ref[here(c), width:] = (dprod * b).astype(BF16)
            outer_ref[here(c), width:] = (dx[:, :width] + dprod * af).astype(BF16)
            rows1 = w1_ref.shape[0]
            grad_ref[:rows1, :] += dot_rows(v["x"], v["dpre"])
            grad_ref[rows1:, :] += dot_rows(v["dm"], v["h"])

        stages = [stage0, stage1, stage2, stage3]
        for t in range(chunks + len(stages) - 1):
            for s in ORDER:
                c = t - s
                if 0 <= c < chunks:
                    stages[s](c)
        for copy in keeps(step):
            copy.start()
        return carry

    def scatter(step, sent):
        for j in range(parts):
            part = step * parts + j
            span, hot = window(part, 0)
            total_ref[span, :] += dot(hot, outer_ref[place(part), :])

        @pl.when(most_ref[step] > 1)
        def _():
            for j in range(parts):
                part = step * parts + j

                def more(w, carry):
                    span, hot = window(part, w)
                    total_ref[span, :] += dot(hot, outer_ref[place(part), :])
                    return carry

                lax.fori_loop(1, count_ref[part], more, 0)

        steps = trips // BLOCK
        follow = base_ref[jnp.minimum((step + 1) * parts, steps * parts - 1)]
        ready = jnp.where(step == steps - 1, ndev // GROUP, follow // (GROUP * slots_per))
        lax.fori_loop(sent, ready, close, 0)
        return ready

    def leave(q):
        devices = pl.ds(q * GROUP, GROUP)
        return pltpu.make_async_copy(out_ref.at[devices], out_hbm.at[devices], out_sem.at[q])

    def close(q, carry):
        for i in range(GROUP):
            d = q * GROUP + i
            sums = total_ref[pl.ds(pl.multiple_of(d * slots_per, slots_per), slots_per), :]
            out_ref[d, :slots_per, :] = sums[:, :width].astype(BF16)
            out_ref[d, slots_per : 2 * slots_per, :] = sums[:, width:].astype(BF16)
        leave(q).start()
        return carry

    def close_grad(k, carry):
        for c in range(2):
            g = grad_ref[pl.ds(pl.multiple_of(k * 8, 8), 8), c * 128 : (c + 1) * 128]
            out_ref[2 * k + c, 2 * slots_per :, :] = g.astype(BF16)
        return carry

    lax.fori_loop(0, trips // BLOCK, gather, 0)
    lax.fori_loop(0, trips // SUPER, mlp, 0)
    lax.fori_loop(0, ndev // 2, close_grad, 0, unroll=4)
    lax.fori_loop(0, trips // BLOCK, scatter, 0)
    for q in range(ndev // GROUP):
        leave(q).wait()
    for step in range(trips // SUPER):
        for copy in keeps(step):
            copy.wait()


def triplets(remote, own, far, w1, bias, w2, ndev):
    trips = remote.shape[0]
    slots, pair = far.shape
    width = pair // 2
    hid = w1.shape[1]
    rows1 = w1.shape[0]
    steps = trips // BLOCK
    parts = BLOCK // PART
    blocks = remote.reshape(steps * parts, PART)
    base = jnp.minimum(blocks[:, 0] // 16 * 16, slots - WINDOW)
    count = (blocks[:, PART - 1] - base) // WINDOW + 1
    most = jnp.max(count.reshape(steps, parts), axis=1)
    row = remote.reshape(steps * parts, 1, PART)
    smem = pl.BlockSpec(memory_space=pltpu.SMEM)
    vmem = pl.BlockSpec(memory_space=pltpu.VMEM)
    hbm = pl.BlockSpec(memory_space=pltpu.HBM)
    return pl.pallas_call(
        triplet_kernel,
        in_specs=[smem] * 3 + [vmem, hbm] + [vmem] * 6,
        out_specs=[hbm, hbm, hbm, vmem],
        scratch_shapes=[
            pltpu.VMEM((slots, pair), F32),
            pltpu.VMEM((rows1 + width, hid), F32),
            pltpu.VMEM((trips, pair), BF16),
            pltpu.VMEM((trips, pair), BF16),
            pltpu.VMEM((trips, pair), BF16),
            pltpu.VMEM((trips, pair), BF16),
            pltpu.VMEM((trips, hid), BF16),
            pltpu.VMEM((ndev, 2 * slots // ndev + 8, width), BF16),
            pltpu.SemaphoreType.DMA((trips // SUPER,)),
            pltpu.SemaphoreType.DMA((2, trips // SUPER)),
            pltpu.SemaphoreType.DMA((ndev // GROUP,)),
        ],
        out_shape=[
            pltpu.HBM((trips, pair), BF16),
            pltpu.HBM((trips, hid), BF16),
            pltpu.HBM((ndev, 2 * slots // ndev + 8, width), BF16),
            jax.ShapeDtypeStruct((1, hid), F32),
        ],
        compiler_params=pltpu.CompilerParams(vmem_limit_bytes=36 * 2**20),
        cost_estimate=pl.CostEstimate(
            flops=2 * trips * 600000, bytes_accessed=20 * 2**20, transcendentals=trips * hid
        ),
        name="triplets",
    )(base, count, most, row, pltpu.with_memory_space_constraint(own, pltpu.HBM), far, w1, w1[width:].T, w2, w2.T, bias[None, :])


def pack_kernel(
    edges_hbm,
    cot_hbm,
    rows_hbm,
    count_hbm,
    table_hbm,
    out_hbm,
    rows_ref,
    count_ref,
    table_ref,
    index_ref,
    out_ref,
    in_sem,
    table_sem,
    out_sem,
):
    rows, width = edges_hbm.shape
    fetches = [
        pltpu.make_async_copy(rows_hbm, rows_ref, in_sem.at[0]),
        pltpu.make_async_copy(count_hbm, count_ref, in_sem.at[1]),
        pltpu.make_async_copy(edges_hbm, table_ref.at[:, pl.ds(0, width)], in_sem.at[2]),
        pltpu.make_async_copy(cot_hbm, table_ref.at[:, pl.ds(width, width)], in_sem.at[3]),
    ]
    for copy in fetches:
        copy.start()
    slots_per, ndev = rows_ref.shape
    block = out_ref.shape[1]
    group = block // slots_per
    fetches[0].wait()
    fetches[1].wait()
    slot = lax.broadcasted_iota(jnp.int32, (slots_per, ndev), 0)
    chosen = jnp.where(slot < count_ref[...], rows_ref[...], -1)
    for d in range(ndev):
        index_ref[d // group, (d % group) * slots_per : (d % group + 1) * slots_per, :] = (
            jnp.broadcast_to(chosen[:, d : d + 1], (slots_per, 128))
        )

    fetches[2].wait()
    fetches[3].wait()
    keep = pltpu.make_async_copy(table_ref, table_hbm, table_sem)
    keep.start()

    def send(g):
        start = pl.multiple_of(g * block, block)
        return pltpu.make_async_copy(out_ref.at[g], out_hbm.at[pl.ds(start, block)], out_sem.at[g])

    def body(g, carry):
        index = index_ref[g]
        lane = lax.broadcasted_iota(jnp.int32, index.shape, 1)
        hot = jnp.concatenate(
            [(index == lane + k * 128).astype(F32).astype(BF16) for k in range(rows // 128)], axis=1
        )
        out_ref[g] = dot(hot, table_ref[...]).astype(BF16)
        send(g).start()
        return carry

    groups = out_ref.shape[0]
    lax.fori_loop(0, groups, body, 0)
    for g in range(groups):
        send(g).wait()
    keep.wait()


def pack(edges, cotangent, rows_t, count):
    rows, width = edges.shape
    slots_per, ndev = rows_t.shape
    slots = slots_per * ndev
    groups = slots // PACK
    hbm = pl.BlockSpec(memory_space=pltpu.HBM)
    args = [pltpu.with_memory_space_constraint(v, pltpu.HBM) for v in (edges, cotangent, rows_t, count)]
    return pl.pallas_call(
        pack_kernel,
        in_specs=[hbm] * 4,
        out_specs=[hbm] * 2,
        out_shape=[
            pltpu.HBM((rows, 2 * width), BF16),
            pltpu.HBM((slots, 2 * width), BF16),
        ],
        scratch_shapes=[
            pltpu.VMEM((slots_per, ndev), jnp.int32),
            pltpu.VMEM((1, ndev), jnp.int32),
            pltpu.VMEM((rows, 2 * width), BF16),
            pltpu.VMEM((groups, PACK, 128), jnp.int32),
            pltpu.VMEM((groups, PACK, 2 * width), BF16),
            pltpu.SemaphoreType.DMA((4,)),
            pltpu.SemaphoreType.DMA,
            pltpu.SemaphoreType.DMA((groups,)),
        ],
        compiler_params=pltpu.CompilerParams(vmem_limit_bytes=36 * 2**20),
        cost_estimate=pl.CostEstimate(
            flops=4 * slots * rows * width, bytes_accessed=4 * 2**20, transcendentals=0
        ),
        name="pack",
    )(*args)


def unpack_kernel(shared_ref, first_ref, bias_ref, second_ref):
    width = shared_ref.shape[2] // 2
    cut = first_ref.shape[0] // 8
    for k in range(cut):
        for c in range(2):
            first_ref[8 * k : 8 * k + 8, c * width : (c + 1) * width] = shared_ref[
                2 * k + c, :, :width
            ].astype(F32)
    rest = shared_ref.shape[0] // 2 - cut
    for c in range(2):
        tall = jnp.concatenate(
            [shared_ref[2 * (cut + k) + c, :, :width].astype(F32) for k in range(rest)], axis=0
        )
        second_ref[c * width : (c + 1) * width, :] = tall.T
    ends = jnp.sum(shared_ref[:, :, width:].astype(F32), axis=0)
    for c in range(2):
        bias_ref[:, c * width : (c + 1) * width] = ends[c : c + 1, :] + ends[c + 2 : c + 3, :]


def unpack(shared, rows1, hid, width):
    vmem = pl.BlockSpec(memory_space=pltpu.VMEM)
    return pl.pallas_call(
        unpack_kernel,
        in_specs=[vmem],
        out_specs=[vmem] * 3,
        out_shape=[
            jax.ShapeDtypeStruct((rows1, hid), F32),
            jax.ShapeDtypeStruct((1, hid), F32),
            jax.ShapeDtypeStruct((hid, width), F32),
        ],
        cost_estimate=pl.CostEstimate(flops=0, bytes_accessed=2**20, transcendentals=0),
        name="unpack",
    )(pltpu.with_memory_space_constraint(shared, pltpu.VMEM))


def split(x):
    high = lax.reduce_precision(x, 8, 7)
    return high.astype(BF16), (x - high).astype(BF16)


def local(
    edges, cotangent, send_rows, send_count, trip_local, trip_remote, w_first, bias_first, w_second
):
    width = edges.shape[1]
    rows = edges.shape[0]
    ndev = lax.axis_size("phi") * lax.axis_size("eta")
    slots_per = send_rows.shape[2]
    slots = ndev * slots_per
    pair = 2 * width
    live = jnp.arange(slots_per, dtype=jnp.int32)[None, :] < send_count[0][:, None]
    chosen = jnp.where(live, send_rows[0], -1).reshape(slots)
    row_ids = jnp.arange(rows, dtype=jnp.int32)
    table, outgoing = pack(edges, cotangent, send_rows[0].T, send_count)
    outgoing = outgoing.reshape(ndev, slots_per, pair)
    arrived = lax.all_to_all(outgoing, AXES, split_axis=0, concat_axis=0, tiled=True)
    arrived = arrived.reshape(slots, pair)
    with jax.named_scope("order"):
        key = jnp.sort(trip_remote * rows + trip_local)
        remote = key // rows
        inner = key - remote * rows
    with jax.named_scope("own_rows"):
        own = dot((inner[:, None] == row_ids[None, :]).astype(BF16), table).astype(BF16)
    kept, dpre, outbound, gbias = triplets(
        remote, own, arrived, w_first, bias_first, w_second, ndev
    )
    returned = lax.all_to_all(outbound, AXES, split_axis=0, concat_axis=0, tiled=True)
    with jax.named_scope("own_sums"):
        d_inner = dot(dpre, w_first[:width].T) + kept[:, width:].astype(F32)
        inner_sums = jnp.concatenate([kept[:, :width], d_inner.astype(BF16)], axis=1)
        own_sum = dot((row_ids[:, None] == inner[None, :]).astype(BF16), inner_sums)
        own_sum = lax.optimization_barrier(table.astype(F32) + own_sum)
    hid = w_first.shape[1]
    mine = jnp.sum(returned[:, 2 * slots_per :, :].astype(F32), axis=0).astype(BF16)
    bias_high, bias_low = split(gbias)
    ends = jnp.concatenate([bias_high, bias_low], axis=0).reshape(4, width)
    ends = jnp.pad(ends, ((0, 4), (0, 0)))
    share = jnp.concatenate([mine, ends], axis=1)
    share = jnp.broadcast_to(share[None], (ndev,) + share.shape)
    shared = lax.all_to_all(share, AXES, split_axis=0, concat_axis=0, tiled=True)
    with jax.named_scope("far_sums"):
        back = jnp.concatenate(
            [returned[:, :slots_per, :], returned[:, slots_per : 2 * slots_per, :]], axis=2
        ).reshape(slots, pair)
        far_sum = dot((row_ids[:, None] == chosen[None, :]).astype(BF16), back)
    both = (own_sum + far_sum).astype(BF16)
    grad_first, grad_bias, grad_second = unpack(shared, w_first.shape[0], hid, width)
    return (both[:, :width], both[:, width:], grad_first, grad_bias.reshape(hid), grad_second)


def solution(mesh):
    in_specs = (
        P(AXES, None),
        P(AXES, None),
        P(AXES, None, None),
        P(AXES, None),
        P(AXES),
        P(AXES),
        P(),
        P(),
        P(),
    )
    out_specs = (P(AXES, None), P(AXES, None), P(), P(), P())
    return jax.shard_map(local, mesh=mesh, in_specs=in_specs, out_specs=out_specs, check_vma=False)
```

```python
import functools

import jax
import jax.numpy as jnp
from jax import lax
from jax.experimental import pallas as pl
from jax.experimental.pallas import tpu as pltpu
from jax.sharding import PartitionSpec as P

AXES = ("phi", "eta")
BLOCK = 4096
GROUP = 16
PACK = 512
SUPER = 4096
CHUNK = 512
ORDER = (3, 2, 1, 0)
PART = 256
WINDOW = 256
BF16 = jnp.bfloat16
F32 = jnp.float32


def dot(a, b):
    return jnp.dot(a, b, preferred_element_type=F32)


def dot_rows(a, b):
    return lax.dot_general(a, b, (((0,), (0,)), ((), ())), preferred_element_type=F32)


def triplet_kernel(
    base_ref,
    count_ref,
    most_ref,
    row_ref,
    own_hbm,
    far_ref,
    w1_ref,
    w1t_ref,
    w2_ref,
    w2t_ref,
    bias_ref,
    inner_hbm,
    dpre_hbm,
    out_hbm,
    gbias_ref,
    total_ref,
    grad_ref,
    far2_ref,
    outer_ref,
    own_ref,
    inner_ref,
    dpre_ref,
    out_ref,
    own_sem,
    keep_sem,
    out_sem,
):
    trips = own_ref.shape[0]

    def fetch(step):
        rows = pl.ds(pl.multiple_of(step * SUPER, SUPER), SUPER)
        return pltpu.make_async_copy(own_hbm.at[rows], own_ref.at[rows], own_sem.at[step])

    for step in range(trips // SUPER):
        fetch(step).start()
    width = own_ref.shape[1] // 2
    slots = far_ref.shape[0]
    parts = BLOCK // PART
    ndev = out_ref.shape[0]
    slots_per = slots // ndev

    total_ref[...] = jnp.zeros_like(total_ref)
    grad_ref[...] = jnp.zeros_like(grad_ref)
    gbias_ref[...] = jnp.zeros_like(gbias_ref)

    def window(part, w):
        first = base_ref[part] + w * WINDOW
        start = pl.multiple_of(jnp.minimum(first, slots - WINDOW), 16)
        rel = row_ref[part] - start
        if not isinstance(w, int):
            rel = jnp.where(rel >= first - start, rel, -1)
        down = lax.broadcasted_iota(jnp.int32, (WINDOW, PART), 0)
        return pl.ds(start, WINDOW), (down == rel).astype(F32).astype(BF16)

    def place(part):
        return pl.ds(pl.multiple_of(part * PART, PART), PART)

    def gather(step, carry):
        for j in range(parts):
            part = step * parts + j
            span, hot = window(part, 0)
            far2_ref[place(part), :] = dot_rows(hot, far_ref[span, :]).astype(BF16)

        @pl.when(most_ref[step] > 1)
        def _():
            for j in range(parts):
                part = step * parts + j

                def more(w, carry):
                    span, hot = window(part, w)
                    far2_ref[place(part), :] += dot_rows(hot, far_ref[span, :]).astype(BF16)
                    return carry

                lax.fori_loop(1, count_ref[part], more, 0)

        return carry

    def keeps(step):
        rows = pl.ds(pl.multiple_of(step * SUPER, SUPER), SUPER)
        return (
            pltpu.make_async_copy(inner_ref.at[rows], inner_hbm.at[rows], keep_sem.at[0, step]),
            pltpu.make_async_copy(dpre_ref.at[rows], dpre_hbm.at[rows], keep_sem.at[1, step]),
        )

    def mlp(step, carry):
        fetch(step).wait()
        chunks = SUPER // CHUNK
        state = [dict() for _ in range(chunks)]

        def here(c):
            return pl.ds(pl.multiple_of(step * SUPER + c * CHUNK, CHUNK), CHUNK)

        def stage0(c):
            v = state[c]
            a = own_ref[here(c), :width]
            b = far2_ref[here(c), :width]
            prod = (a.astype(F32) * b.astype(F32)).astype(BF16)
            v["x"] = jnp.concatenate([a, b, prod], axis=1)
            v["pre"] = dot(v["x"], w1_ref[...]) + bias_ref[...]
            ga = own_ref[here(c), width:]
            gb = far2_ref[here(c), width:]
            v["dm"] = (ga.astype(F32) + gb.astype(F32)).astype(BF16)
            v["dh"] = dot(v["dm"], w2t_ref[...])

        def stage1(c):
            v = state[c]
            pre = v.pop("pre")
            sig = 0.5 * jnp.tanh(0.5 * pre) + 0.5
            v["h"] = (pre * sig).astype(BF16)
            dpre = v.pop("dh") * (sig * (1.0 + pre * (1.0 - sig)))
            gbias_ref[...] += jnp.sum(dpre, axis=0, keepdims=True)
            v["dpre"] = dpre.astype(BF16)
            dpre_ref[here(c), :] = v["dpre"]

        def stage2(c):
            v = state[c]
            mb = dot(v["h"], w2_ref[...]).astype(BF16)
            inner_ref[here(c), :width] = mb
            outer_ref[here(c), :width] = mb
            v["dx"] = dot(v["dpre"], w1t_ref[...])

        def stage3(c):
            v = state[c]
            dx = v.pop("dx")
            af = own_ref[here(c), :width].astype(F32)
            b = far2_ref[here(c), :width].astype(F32)
            dprod = dx[:, width:]
            inner_ref[here(c), width:] = (dprod * b).astype(BF16)
            outer_ref[here(c), width:] = (dx[:, :width] + dprod * af).astype(BF16)
            rows1 = w1_ref.shape[0]
            grad_ref[:rows1, :] += dot_rows(v["x"], v["dpre"])
            grad_ref[rows1:, :] += dot_rows(v["dm"], v["h"])

        stages = [stage0, stage1, stage2, stage3]
        for t in range(chunks + len(stages) - 1):
            for s in ORDER:
                c = t - s
                if 0 <= c < chunks:
                    stages[s](c)
        for copy in keeps(step):
            copy.start()
        return carry

    def scatter(step, sent):
        for j in range(parts):
            part = step * parts + j
            span, hot = window(part, 0)
            total_ref[span, :] += dot(hot, outer_ref[place(part), :])

        @pl.when(most_ref[step] > 1)
        def _():
            for j in range(parts):
                part = step * parts + j

                def more(w, carry):
                    span, hot = window(part, w)
                    total_ref[span, :] += dot(hot, outer_ref[place(part), :])
                    return carry

                lax.fori_loop(1, count_ref[part], more, 0)

        steps = trips // BLOCK
        follow = base_ref[jnp.minimum((step + 1) * parts, steps * parts - 1)]
        ready = jnp.where(step == steps - 1, ndev // GROUP, follow // (GROUP * slots_per))
        lax.fori_loop(sent, ready, close, 0)
        return ready

    def leave(q):
        devices = pl.ds(q * GROUP, GROUP)
        return pltpu.make_async_copy(out_ref.at[devices], out_hbm.at[devices], out_sem.at[q])

    def close(q, carry):
        for i in range(GROUP):
            d = q * GROUP + i
            sums = total_ref[pl.ds(pl.multiple_of(d * slots_per, slots_per), slots_per), :]
            out_ref[d, :slots_per, :] = sums[:, :width].astype(BF16)
            out_ref[d, slots_per : 2 * slots_per, :] = sums[:, width:].astype(BF16)
        leave(q).start()
        return carry

    def close_grad(k, carry):
        for c in range(2):
            g = grad_ref[pl.ds(pl.multiple_of(k * 8, 8), 8), c * 128 : (c + 1) * 128]
            out_ref[2 * k + c, 2 * slots_per :, :] = g.astype(BF16)
        return carry

    lax.fori_loop(0, trips // BLOCK, gather, 0)
    lax.fori_loop(0, trips // SUPER, mlp, 0)
    lax.fori_loop(0, ndev // 2, close_grad, 0, unroll=4)
    lax.fori_loop(0, trips // BLOCK, scatter, 0)
    for q in range(ndev // GROUP):
        leave(q).wait()
    for step in range(trips // SUPER):
        for copy in keeps(step):
            copy.wait()


def triplets(remote, own, far, w1, bias, w2, ndev):
    trips = remote.shape[0]
    slots, pair = far.shape
    width = pair // 2
    hid = w1.shape[1]
    rows1 = w1.shape[0]
    steps = trips // BLOCK
    parts = BLOCK // PART
    blocks = remote.reshape(steps * parts, PART)
    base = jnp.minimum(blocks[:, 0] // 16 * 16, slots - WINDOW)
    count = (blocks[:, PART - 1] - base) // WINDOW + 1
    most = jnp.max(count.reshape(steps, parts), axis=1)
    row = remote.reshape(steps * parts, 1, PART)
    smem = pl.BlockSpec(memory_space=pltpu.SMEM)
    vmem = pl.BlockSpec(memory_space=pltpu.VMEM)
    hbm = pl.BlockSpec(memory_space=pltpu.HBM)
    return pl.pallas_call(
        triplet_kernel,
        in_specs=[smem] * 3 + [vmem, hbm] + [vmem] * 6,
        out_specs=[hbm, hbm, hbm, vmem],
        scratch_shapes=[
            pltpu.VMEM((slots, pair), F32),
            pltpu.VMEM((rows1 + width, hid), F32),
            pltpu.VMEM((trips, pair), BF16),
            pltpu.VMEM((trips, pair), BF16),
            pltpu.VMEM((trips, pair), BF16),
            pltpu.VMEM((trips, pair), BF16),
            pltpu.VMEM((trips, hid), BF16),
            pltpu.VMEM((ndev, 2 * slots // ndev + 8, width), BF16),
            pltpu.SemaphoreType.DMA((trips // SUPER,)),
            pltpu.SemaphoreType.DMA((2, trips // SUPER)),
            pltpu.SemaphoreType.DMA((ndev // GROUP,)),
        ],
        out_shape=[
            pltpu.HBM((trips, pair), BF16),
            pltpu.HBM((trips, hid), BF16),
            pltpu.HBM((ndev, 2 * slots // ndev + 8, width), BF16),
            jax.ShapeDtypeStruct((1, hid), F32),
        ],
        compiler_params=pltpu.CompilerParams(vmem_limit_bytes=36 * 2**20),
        cost_estimate=pl.CostEstimate(
            flops=2 * trips * 600000, bytes_accessed=20 * 2**20, transcendentals=trips * hid
        ),
        name="triplets",
    )(base, count, most, row, pltpu.with_memory_space_constraint(own, pltpu.HBM), far, w1, w1[width:].T, w2, w2.T, bias[None, :])


def pack_kernel(
    edges_hbm,
    cot_hbm,
    rows_hbm,
    count_hbm,
    table_hbm,
    out_hbm,
    rows_ref,
    count_ref,
    table_ref,
    index_ref,
    out_ref,
    in_sem,
    table_sem,
    out_sem,
):
    rows, width = edges_hbm.shape
    fetches = [
        pltpu.make_async_copy(rows_hbm, rows_ref, in_sem.at[0]),
        pltpu.make_async_copy(count_hbm, count_ref, in_sem.at[1]),
        pltpu.make_async_copy(edges_hbm, table_ref.at[:, pl.ds(0, width)], in_sem.at[2]),
        pltpu.make_async_copy(cot_hbm, table_ref.at[:, pl.ds(width, width)], in_sem.at[3]),
    ]
    for copy in fetches:
        copy.start()
    slots_per, ndev = rows_ref.shape
    block = out_ref.shape[1]
    group = block // slots_per
    fetches[0].wait()
    fetches[1].wait()
    slot = lax.broadcasted_iota(jnp.int32, (slots_per, ndev), 0)
    chosen = jnp.where(slot < count_ref[...], rows_ref[...], -1)
    for d in range(ndev):
        index_ref[d // group, (d % group) * slots_per : (d % group + 1) * slots_per, :] = (
            jnp.broadcast_to(chosen[:, d : d + 1], (slots_per, 128))
        )

    fetches[2].wait()
    fetches[3].wait()
    keep = pltpu.make_async_copy(table_ref, table_hbm, table_sem)
    keep.start()

    def send(g):
        start = pl.multiple_of(g * block, block)
        return pltpu.make_async_copy(out_ref.at[g], out_hbm.at[pl.ds(start, block)], out_sem.at[g])

    def body(g, carry):
        index = index_ref[g]
        lane = lax.broadcasted_iota(jnp.int32, index.shape, 1)
        total = None
        for k in range(0, rows, 256):
            hot = jnp.concatenate(
                [(index == lane + (k + c)).astype(F32).astype(BF16) for c in (0, 128)], axis=1
            )
            term = dot(hot, table_ref[k : k + 256, :])
            total = term if total is None else total + term
        out_ref[g] = total.astype(BF16)
        send(g).start()
        return carry

    groups = out_ref.shape[0]
    for g in range(groups):
        body(g, 0)
    for g in range(groups):
        send(g).wait()
    keep.wait()


def pack(edges, cotangent, rows_t, count):
    rows, width = edges.shape
    slots_per, ndev = rows_t.shape
    slots = slots_per * ndev
    groups = slots // PACK
    hbm = pl.BlockSpec(memory_space=pltpu.HBM)
    args = [pltpu.with_memory_space_constraint(v, pltpu.HBM) for v in (edges, cotangent, rows_t, count)]
    return pl.pallas_call(
        pack_kernel,
        in_specs=[hbm] * 4,
        out_specs=[hbm] * 2,
        out_shape=[
            pltpu.HBM((rows, 2 * width), BF16),
            pltpu.HBM((slots, 2 * width), BF16),
        ],
        scratch_shapes=[
            pltpu.VMEM((slots_per, ndev), jnp.int32),
            pltpu.VMEM((1, ndev), jnp.int32),
            pltpu.VMEM((rows, 2 * width), BF16),
            pltpu.VMEM((groups, PACK, 128), jnp.int32),
            pltpu.VMEM((groups, PACK, 2 * width), BF16),
            pltpu.SemaphoreType.DMA((4,)),
            pltpu.SemaphoreType.DMA,
            pltpu.SemaphoreType.DMA((groups,)),
        ],
        compiler_params=pltpu.CompilerParams(vmem_limit_bytes=36 * 2**20),
        cost_estimate=pl.CostEstimate(
            flops=4 * slots * rows * width, bytes_accessed=4 * 2**20, transcendentals=0
        ),
        name="pack",
    )(*args)


def unpack_kernel(shared_ref, first_ref, bias_ref, second_ref):
    width = shared_ref.shape[3]
    cut = first_ref.shape[0] // 8

    def piece(k, c):
        d = 2 * k + c
        return jnp.concatenate([shared_ref[d, 0], shared_ref[d, 1]], axis=0).astype(F32)

    for k in range(cut):
        for c in range(2):
            first_ref[8 * k : 8 * k + 8, c * width : (c + 1) * width] = piece(k, c)
    rest = shared_ref.shape[0] // 2 - cut
    for c in range(2):
        tall = jnp.concatenate([piece(cut + k, c) for k in range(rest)], axis=0)
        second_ref[c * width : (c + 1) * width, :] = tall.T
    ends = jnp.sum(shared_ref[:, 2].astype(F32), axis=0)
    for c in range(2):
        bias_ref[:, c * width : (c + 1) * width] = ends[c : c + 1, :] + ends[c + 2 : c + 3, :]


def unpack(shared, rows1, hid, width):
    vmem = pl.BlockSpec(memory_space=pltpu.VMEM)
    return pl.pallas_call(
        unpack_kernel,
        in_specs=[vmem],
        out_specs=[vmem] * 3,
        out_shape=[
            jax.ShapeDtypeStruct((rows1, hid), F32),
            jax.ShapeDtypeStruct((1, hid), F32),
            jax.ShapeDtypeStruct((hid, width), F32),
        ],
        cost_estimate=pl.CostEstimate(flops=0, bytes_accessed=2**20, transcendentals=0),
        name="unpack",
    )(pltpu.with_memory_space_constraint(shared, pltpu.VMEM))


def split(x):
    high = lax.reduce_precision(x, 8, 7)
    return high.astype(BF16), (x - high).astype(BF16)


def local(
    edges, cotangent, send_rows, send_count, trip_local, trip_remote, w_first, bias_first, w_second
):
    width = edges.shape[1]
    rows = edges.shape[0]
    ndev = lax.axis_size("phi") * lax.axis_size("eta")
    slots_per = send_rows.shape[2]
    slots = ndev * slots_per
    pair = 2 * width
    live = jnp.arange(slots_per, dtype=jnp.int32)[None, :] < send_count[0][:, None]
    chosen = jnp.where(live, send_rows[0], -1).reshape(slots)
    row_ids = jnp.arange(rows, dtype=jnp.int32)
    table, outgoing = pack(edges, cotangent, send_rows[0].T, send_count)
    outgoing = outgoing.reshape(ndev, slots_per, pair)
    arrived = lax.all_to_all(outgoing, AXES, split_axis=0, concat_axis=0, tiled=True)
    arrived = arrived.reshape(slots, pair)
    with jax.named_scope("order"):
        key = jnp.sort(trip_remote * rows + trip_local)
        remote = key // rows
        inner = key - remote * rows
    with jax.named_scope("own_rows"):
        own = dot((inner[:, None] == row_ids[None, :]).astype(BF16), table).astype(BF16)
    kept, dpre, outbound, gbias = triplets(
        remote, own, arrived, w_first, bias_first, w_second, ndev
    )
    returned = lax.all_to_all(outbound, AXES, split_axis=0, concat_axis=0, tiled=True)
    with jax.named_scope("own_sums"):
        d_inner = dot(dpre, w_first[:width].T) + kept[:, width:].astype(F32)
        inner_sums = jnp.concatenate([kept[:, :width], d_inner.astype(BF16)], axis=1)
        own_sum = dot((row_ids[:, None] == inner[None, :]).astype(BF16), inner_sums)
        own_sum = lax.optimization_barrier(table.astype(F32) + own_sum)
    hid = w_first.shape[1]
    mine = jnp.sum(returned[:, 2 * slots_per :, :].astype(F32), axis=0).astype(BF16)
    bias_high, bias_low = split(gbias)
    ends = jnp.concatenate([bias_high, bias_low], axis=0).reshape(1, 4, width)
    share = jnp.concatenate([mine.reshape(2, 4, width), ends], axis=0)
    share = jnp.broadcast_to(share[None], (ndev,) + share.shape)
    shared = lax.all_to_all(share, AXES, split_axis=0, concat_axis=0, tiled=True)
    with jax.named_scope("far_sums"):
        back = jnp.concatenate(
            [returned[:, :slots_per, :], returned[:, slots_per : 2 * slots_per, :]], axis=2
        ).reshape(slots, pair)
        far_sum = dot((row_ids[:, None] == chosen[None, :]).astype(BF16), back)
    both = (own_sum + far_sum).astype(BF16)
    grad_first, grad_bias, grad_second = unpack(shared, w_first.shape[0], hid, width)
    return (both[:, :width], both[:, width:], grad_first, grad_bias.reshape(hid), grad_second)


def solution(mesh):
    in_specs = (
        P(AXES, None),
        P(AXES, None),
        P(AXES, None, None),
        P(AXES, None),
        P(AXES),
        P(AXES),
        P(),
        P(),
        P(),
    )
    out_specs = (P(AXES, None), P(AXES, None), P(), P(), P())
    return jax.shard_map(local, mesh=mesh, in_specs=in_specs, out_specs=out_specs, check_vma=False)
```

```python
import functools

import jax
import jax.numpy as jnp
from jax import lax
from jax.experimental import pallas as pl
from jax.experimental.pallas import tpu as pltpu
from jax.sharding import PartitionSpec as P

AXES = ("phi", "eta")
BLOCK = 4096
GROUP = 16
PACK = 512
SUPER = 4096
CHUNK = 512
ORDER = (3, 2, 1, 0)
PART = 256
WINDOW = 256
BF16 = jnp.bfloat16
F32 = jnp.float32


def dot(a, b):
    return jnp.dot(a, b, preferred_element_type=F32)


def dot_rows(a, b):
    return lax.dot_general(a, b, (((0,), (0,)), ((), ())), preferred_element_type=F32)


def triplet_kernel(
    base_ref,
    count_ref,
    most_ref,
    row_ref,
    own_hbm,
    far_ref,
    w1_ref,
    w1t_ref,
    w2_ref,
    w2t_ref,
    bias_ref,
    inner_hbm,
    dpre_hbm,
    out_hbm,
    gbias_ref,
    total_ref,
    grad_ref,
    far2_ref,
    outer_ref,
    own_ref,
    inner_ref,
    dpre_ref,
    out_ref,
    own_sem,
    keep_sem,
    out_sem,
):
    trips = own_ref.shape[0]

    def fetch(step):
        rows = pl.ds(pl.multiple_of(step * SUPER, SUPER), SUPER)
        return pltpu.make_async_copy(own_hbm.at[rows], own_ref.at[rows], own_sem.at[step])

    for step in range(trips // SUPER):
        fetch(step).start()
    width = own_ref.shape[1] // 2
    slots = far_ref.shape[0]
    parts = BLOCK // PART
    ndev = out_ref.shape[0]
    slots_per = slots // ndev

    grad_ref[...] = jnp.zeros_like(grad_ref)
    gbias_ref[...] = jnp.zeros_like(gbias_ref)

    def window(part, w):
        first = base_ref[part] + w * WINDOW
        start = pl.multiple_of(jnp.minimum(first, slots - WINDOW), 16)
        rel = row_ref[part] - start
        if not isinstance(w, int):
            rel = jnp.where(rel >= first - start, rel, -1)
        down = lax.broadcasted_iota(jnp.int32, (WINDOW, PART), 0)
        return pl.ds(start, WINDOW), (down == rel).astype(F32).astype(BF16)

    def place(part):
        return pl.ds(pl.multiple_of(part * PART, PART), PART)

    zone = slots * PART // trips

    def gather(step, carry):
        for j in range(parts):
            part = step * parts + j
            span, hot = window(part, 0)
            far2_ref[place(part), :] = dot_rows(hot, far_ref[span, :]).astype(BF16)
            blank = pl.ds(pl.multiple_of(part * zone, zone), zone)
            total_ref[blank, :] = jnp.zeros((zone, 2 * width), F32)

        @pl.when(most_ref[step] > 1)
        def _():
            for j in range(parts):
                part = step * parts + j

                def more(w, carry):
                    span, hot = window(part, w)
                    far2_ref[place(part), :] += dot_rows(hot, far_ref[span, :]).astype(BF16)
                    return carry

                lax.fori_loop(1, count_ref[part], more, 0)

        return carry

    def keeps(step):
        rows = pl.ds(pl.multiple_of(step * SUPER, SUPER), SUPER)
        return (
            pltpu.make_async_copy(inner_ref.at[rows], inner_hbm.at[rows], keep_sem.at[0, step]),
            pltpu.make_async_copy(dpre_ref.at[rows], dpre_hbm.at[rows], keep_sem.at[1, step]),
        )

    def mlp(step, carry):
        fetch(step).wait()
        chunks = SUPER // CHUNK
        state = [dict() for _ in range(chunks)]

        def here(c):
            return pl.ds(pl.multiple_of(step * SUPER + c * CHUNK, CHUNK), CHUNK)

        def stage0(c):
            v = state[c]
            a = own_ref[here(c), :width]
            b = far2_ref[here(c), :width]
            prod = (a.astype(F32) * b.astype(F32)).astype(BF16)
            v["x"] = jnp.concatenate([a, b, prod], axis=1)
            v["pre"] = dot(v["x"], w1_ref[...]) + bias_ref[...]
            ga = own_ref[here(c), width:]
            gb = far2_ref[here(c), width:]
            v["dm"] = (ga.astype(F32) + gb.astype(F32)).astype(BF16)
            v["dh"] = dot(v["dm"], w2t_ref[...])

        def stage1(c):
            v = state[c]
            pre = v.pop("pre")
            sig = 0.5 * jnp.tanh(0.5 * pre) + 0.5
            v["h"] = (pre * sig).astype(BF16)
            dpre = v.pop("dh") * (sig * (1.0 + pre * (1.0 - sig)))
            gbias_ref[...] += jnp.sum(dpre, axis=0, keepdims=True)
            v["dpre"] = dpre.astype(BF16)
            dpre_ref[here(c), :] = v["dpre"]

        def stage2(c):
            v = state[c]
            mb = dot(v["h"], w2_ref[...]).astype(BF16)
            inner_ref[here(c), :width] = mb
            outer_ref[here(c), :width] = mb
            v["dx"] = dot(v["dpre"], w1t_ref[...])
            rows1 = w1_ref.shape[0]
            grad_ref[:rows1, :] += dot_rows(v["x"], v["dpre"])
            grad_ref[rows1:, :] += dot_rows(v["dm"], v["h"])

        def stage3(c):
            v = state[c]
            dx = v.pop("dx")
            af = own_ref[here(c), :width].astype(F32)
            b = far2_ref[here(c), :width].astype(F32)
            dprod = dx[:, width:]
            inner_ref[here(c), width:] = (dprod * b).astype(BF16)
            outer_ref[here(c), width:] = (dx[:, :width] + dprod * af).astype(BF16)

        stages = [stage0, stage1, stage2, stage3]
        for t in range(chunks + len(stages) - 1):
            for s in ORDER:
                c = t - s
                if 0 <= c < chunks:
                    stages[s](c)
        for copy in keeps(step):
            copy.start()
        return carry

    def scatter(step, sent):
        for j in range(parts):
            part = step * parts + j
            span, hot = window(part, 0)
            total_ref[span, :] += dot(hot, outer_ref[place(part), :])

        @pl.when(most_ref[step] > 1)
        def _():
            for j in range(parts):
                part = step * parts + j

                def more(w, carry):
                    span, hot = window(part, w)
                    total_ref[span, :] += dot(hot, outer_ref[place(part), :])
                    return carry

                lax.fori_loop(1, count_ref[part], more, 0)

        steps = trips // BLOCK
        follow = base_ref[jnp.minimum((step + 1) * parts, steps * parts - 1)]
        ready = jnp.where(step == steps - 1, ndev // GROUP, follow // (GROUP * slots_per))
        lax.fori_loop(sent, ready, close, 0)
        return ready

    def leave(q):
        devices = pl.ds(q * GROUP, GROUP)
        return pltpu.make_async_copy(out_ref.at[devices], out_hbm.at[devices], out_sem.at[q])

    def close(q, carry):
        for i in range(GROUP):
            d = q * GROUP + i
            sums = total_ref[pl.ds(pl.multiple_of(d * slots_per, slots_per), slots_per), :]
            out_ref[d, :slots_per, :] = sums[:, :width].astype(BF16)
            out_ref[d, slots_per : 2 * slots_per, :] = sums[:, width:].astype(BF16)
        leave(q).start()
        return carry

    def close_grad(k, carry):
        for c in range(2):
            g = grad_ref[pl.ds(pl.multiple_of(k * 8, 8), 8), c * 128 : (c + 1) * 128]
            out_ref[2 * k + c, 2 * slots_per :, :] = g.astype(BF16)
        return carry

    lax.fori_loop(0, trips // BLOCK, gather, 0)
    lax.fori_loop(0, trips // SUPER, mlp, 0)
    lax.fori_loop(0, ndev // 2, close_grad, 0, unroll=4)
    lax.fori_loop(0, trips // BLOCK, scatter, 0)
    for q in range(ndev // GROUP):
        leave(q).wait()
    for step in range(trips // SUPER):
        for copy in keeps(step):
            copy.wait()


def triplets(remote, own, far, w1, bias, w2, ndev):
    trips = remote.shape[0]
    slots, pair = far.shape
    width = pair // 2
    hid = w1.shape[1]
    rows1 = w1.shape[0]
    steps = trips // BLOCK
    parts = BLOCK // PART
    blocks = remote.reshape(steps * parts, PART)
    base = jnp.minimum(blocks[:, 0] // 16 * 16, slots - WINDOW)
    count = (blocks[:, PART - 1] - base) // WINDOW + 1
    most = jnp.max(count.reshape(steps, parts), axis=1)
    row = remote.reshape(steps * parts, 1, PART)
    smem = pl.BlockSpec(memory_space=pltpu.SMEM)
    vmem = pl.BlockSpec(memory_space=pltpu.VMEM)
    hbm = pl.BlockSpec(memory_space=pltpu.HBM)
    return pl.pallas_call(
        triplet_kernel,
        in_specs=[smem] * 3 + [vmem, hbm] + [vmem] * 6,
        out_specs=[hbm, hbm, hbm, vmem],
        scratch_shapes=[
            pltpu.VMEM((slots, pair), F32),
            pltpu.VMEM((rows1 + width, hid), F32),
            pltpu.VMEM((trips, pair), BF16),
            pltpu.VMEM((trips, pair), BF16),
            pltpu.VMEM((trips, pair), BF16),
            pltpu.VMEM((trips, pair), BF16),
            pltpu.VMEM((trips, hid), BF16),
            pltpu.VMEM((ndev, 2 * slots // ndev + 8, width), BF16),
            pltpu.SemaphoreType.DMA((trips // SUPER,)),
            pltpu.SemaphoreType.DMA((2, trips // SUPER)),
            pltpu.SemaphoreType.DMA((ndev // GROUP,)),
        ],
        out_shape=[
            pltpu.HBM((trips, pair), BF16),
            pltpu.HBM((trips, hid), BF16),
            pltpu.HBM((ndev, 2 * slots // ndev + 8, width), BF16),
            jax.ShapeDtypeStruct((1, hid), F32),
        ],
        compiler_params=pltpu.CompilerParams(vmem_limit_bytes=36 * 2**20),
        cost_estimate=pl.CostEstimate(
            flops=2 * trips * 600000, bytes_accessed=20 * 2**20, transcendentals=trips * hid
        ),
        name="triplets",
    )(base, count, most, row, pltpu.with_memory_space_constraint(own, pltpu.HBM), far, w1, w1[width:].T, w2, w2.T, bias[None, :])


def pack_kernel(
    edges_hbm,
    cot_hbm,
    rows_hbm,
    count_hbm,
    table_hbm,
    out_hbm,
    rows_ref,
    count_ref,
    table_ref,
    index_ref,
    out_ref,
    in_sem,
    table_sem,
    out_sem,
):
    rows, width = edges_hbm.shape
    fetches = [
        pltpu.make_async_copy(rows_hbm, rows_ref, in_sem.at[0]),
        pltpu.make_async_copy(count_hbm, count_ref, in_sem.at[1]),
        pltpu.make_async_copy(edges_hbm, table_ref.at[:, pl.ds(0, width)], in_sem.at[2]),
        pltpu.make_async_copy(cot_hbm, table_ref.at[:, pl.ds(width, width)], in_sem.at[3]),
    ]
    for copy in fetches:
        copy.start()
    slots_per, ndev = rows_ref.shape
    block = out_ref.shape[1]
    group = block // slots_per
    fetches[0].wait()
    fetches[1].wait()
    slot = lax.broadcasted_iota(jnp.int32, (slots_per, ndev), 0)
    chosen = jnp.where(slot < count_ref[...], rows_ref[...], -1)
    for d in range(ndev):
        index_ref[d // group, (d % group) * slots_per : (d % group + 1) * slots_per, :] = (
            jnp.broadcast_to(chosen[:, d : d + 1], (slots_per, 128))
        )

    fetches[2].wait()
    fetches[3].wait()
    keep = pltpu.make_async_copy(table_ref, table_hbm, table_sem)
    keep.start()

    def send(g):
        start = pl.multiple_of(g * block, block)
        return pltpu.make_async_copy(out_ref.at[g], out_hbm.at[pl.ds(start, block)], out_sem.at[g])

    def body(g, carry):
        index = index_ref[g]
        lane = lax.broadcasted_iota(jnp.int32, index.shape, 1)
        total = None
        for k in range(0, rows, 256):
            hot = jnp.concatenate(
                [(index == lane + (k + c)).astype(F32).astype(BF16) for c in (0, 128)], axis=1
            )
            term = dot(hot, table_ref[k : k + 256, :])
            total = term if total is None else total + term
        out_ref[g] = total.astype(BF16)
        send(g).start()
        return carry

    groups = out_ref.shape[0]
    for g in range(groups):
        body(g, 0)
    for g in range(groups):
        send(g).wait()
    keep.wait()


def pack(edges, cotangent, rows_t, count):
    rows, width = edges.shape
    slots_per, ndev = rows_t.shape
    slots = slots_per * ndev
    groups = slots // PACK
    hbm = pl.BlockSpec(memory_space=pltpu.HBM)
    args = [pltpu.with_memory_space_constraint(v, pltpu.HBM) for v in (edges, cotangent, rows_t, count)]
    return pl.pallas_call(
        pack_kernel,
        in_specs=[hbm] * 4,
        out_specs=[hbm] * 2,
        out_shape=[
            pltpu.HBM((rows, 2 * width), BF16),
            pltpu.HBM((slots, 2 * width), BF16),
        ],
        scratch_shapes=[
            pltpu.VMEM((slots_per, ndev), jnp.int32),
            pltpu.VMEM((1, ndev), jnp.int32),
            pltpu.VMEM((rows, 2 * width), BF16),
            pltpu.VMEM((groups, PACK, 128), jnp.int32),
            pltpu.VMEM((groups, PACK, 2 * width), BF16),
            pltpu.SemaphoreType.DMA((4,)),
            pltpu.SemaphoreType.DMA,
            pltpu.SemaphoreType.DMA((groups,)),
        ],
        compiler_params=pltpu.CompilerParams(vmem_limit_bytes=36 * 2**20),
        cost_estimate=pl.CostEstimate(
            flops=4 * slots * rows * width, bytes_accessed=4 * 2**20, transcendentals=0
        ),
        name="pack",
    )(*args)


def unpack_kernel(shared_ref, first_ref, bias_ref, second_ref):
    width = shared_ref.shape[3]
    cut = first_ref.shape[0] // 8

    def piece(k, c):
        d = 2 * k + c
        return jnp.concatenate([shared_ref[d, 0], shared_ref[d, 1]], axis=0).astype(F32)

    for k in range(cut):
        for c in range(2):
            first_ref[8 * k : 8 * k + 8, c * width : (c + 1) * width] = piece(k, c)
    rest = shared_ref.shape[0] // 2 - cut
    for c in range(2):
        tall = jnp.concatenate([piece(cut + k, c) for k in range(rest)], axis=0)
        second_ref[c * width : (c + 1) * width, :] = tall.T
    ends = jnp.sum(shared_ref[:, 2].astype(F32), axis=0)
    for c in range(2):
        bias_ref[:, c * width : (c + 1) * width] = ends[c : c + 1, :] + ends[c + 2 : c + 3, :]


def unpack(shared, rows1, hid, width):
    vmem = pl.BlockSpec(memory_space=pltpu.VMEM)
    return pl.pallas_call(
        unpack_kernel,
        in_specs=[vmem],
        out_specs=[vmem] * 3,
        out_shape=[
            jax.ShapeDtypeStruct((rows1, hid), F32),
            jax.ShapeDtypeStruct((1, hid), F32),
            jax.ShapeDtypeStruct((hid, width), F32),
        ],
        cost_estimate=pl.CostEstimate(flops=0, bytes_accessed=2**20, transcendentals=0),
        name="unpack",
    )(pltpu.with_memory_space_constraint(shared, pltpu.VMEM))


def split(x):
    high = lax.reduce_precision(x, 8, 7)
    return high.astype(BF16), (x - high).astype(BF16)


def local(
    edges, cotangent, send_rows, send_count, trip_local, trip_remote, w_first, bias_first, w_second
):
    width = edges.shape[1]
    rows = edges.shape[0]
    ndev = lax.axis_size("phi") * lax.axis_size("eta")
    slots_per = send_rows.shape[2]
    slots = ndev * slots_per
    pair = 2 * width
    live = jnp.arange(slots_per, dtype=jnp.int32)[None, :] < send_count[0][:, None]
    chosen = jnp.where(live, send_rows[0], -1).reshape(slots)
    row_ids = jnp.arange(rows, dtype=jnp.int32)
    table, outgoing = pack(edges, cotangent, send_rows[0].T, send_count)
    outgoing = outgoing.reshape(ndev, slots_per, pair)
    arrived = lax.all_to_all(outgoing, AXES, split_axis=0, concat_axis=0, tiled=True)
    arrived = arrived.reshape(slots, pair)
    with jax.named_scope("order"):
        key = jnp.sort(trip_remote * rows + trip_local)
        remote = key // rows
        inner = key - remote * rows
    with jax.named_scope("own_rows"):
        own = dot((inner[:, None] == row_ids[None, :]).astype(BF16), table).astype(BF16)
    kept, dpre, outbound, gbias = triplets(
        remote, own, arrived, w_first, bias_first, w_second, ndev
    )
    returned = lax.all_to_all(outbound, AXES, split_axis=0, concat_axis=0, tiled=True)
    with jax.named_scope("own_sums"):
        d_inner = dot(dpre, w_first[:width].T) + kept[:, width:].astype(F32)
        inner_sums = jnp.concatenate([kept[:, :width], d_inner.astype(BF16)], axis=1)
        own_sum = dot((row_ids[:, None] == inner[None, :]).astype(BF16), inner_sums)
        own_sum = lax.optimization_barrier(table.astype(F32) + own_sum)
    hid = w_first.shape[1]
    mine = jnp.sum(returned[:, 2 * slots_per :, :].astype(F32), axis=0).astype(BF16)
    bias_high, bias_low = split(gbias)
    ends = jnp.concatenate([bias_high, bias_low], axis=0).reshape(1, 4, width)
    share = jnp.concatenate([mine.reshape(2, 4, width), ends], axis=0)
    share = jnp.broadcast_to(share[None], (ndev,) + share.shape)
    shared = lax.all_to_all(share, AXES, split_axis=0, concat_axis=0, tiled=True)
    with jax.named_scope("far_sums"):
        back = jnp.concatenate(
            [returned[:, :slots_per, :], returned[:, slots_per : 2 * slots_per, :]], axis=2
        ).reshape(slots, pair)
        far_sum = dot((row_ids[:, None] == chosen[None, :]).astype(BF16), back)
    both = (own_sum + far_sum).astype(BF16)
    grad_first, grad_bias, grad_second = unpack(shared, w_first.shape[0], hid, width)
    return (both[:, :width], both[:, width:], grad_first, grad_bias.reshape(hid), grad_second)


def solution(mesh):
    in_specs = (
        P(AXES, None),
        P(AXES, None),
        P(AXES, None, None),
        P(AXES, None),
        P(AXES),
        P(AXES),
        P(),
        P(),
        P(),
    )
    out_specs = (P(AXES, None), P(AXES, None), P(), P(), P())
    return jax.shard_map(local, mesh=mesh, in_specs=in_specs, out_specs=out_specs, check_vma=False)
```

```python
import functools

import jax
import jax.numpy as jnp
from jax import lax
from jax.experimental import pallas as pl
from jax.experimental.pallas import tpu as pltpu
from jax.sharding import PartitionSpec as P

AXES = ("phi", "eta")
BLOCK = 4096
GROUP = 8
PACK = 512
SUPER = 4096
CHUNK = 512
ORDER = (3, 2, 0, 1)
PART = 256
WINDOW = 256
BF16 = jnp.bfloat16
F32 = jnp.float32


def dot(a, b):
    return jnp.dot(a, b, preferred_element_type=F32)


def dot_rows(a, b):
    return lax.dot_general(a, b, (((0,), (0,)), ((), ())), preferred_element_type=F32)


def triplet_kernel(
    base_ref,
    count_ref,
    most_ref,
    row_ref,
    own_hbm,
    far_ref,
    w1_ref,
    w1t_ref,
    w2_ref,
    w2t_ref,
    bias_ref,
    inner_hbm,
    dpre_hbm,
    out_hbm,
    gbias_ref,
    total_ref,
    grad_ref,
    far2_ref,
    outer_ref,
    own_ref,
    inner_ref,
    dpre_ref,
    out_ref,
    own_sem,
    keep_sem,
    out_sem,
):
    trips = own_ref.shape[0]

    def fetch(step):
        rows = pl.ds(pl.multiple_of(step * SUPER, SUPER), SUPER)
        return pltpu.make_async_copy(own_hbm.at[rows], own_ref.at[rows], own_sem.at[step])

    for step in range(trips // SUPER):
        fetch(step).start()
    width = own_ref.shape[1] // 2
    slots = far_ref.shape[0]
    parts = BLOCK // PART
    ndev = out_ref.shape[0]
    slots_per = slots // ndev

    grad_ref[...] = jnp.zeros_like(grad_ref)
    gbias_ref[...] = jnp.zeros_like(gbias_ref)

    def window(part, w):
        first = base_ref[part] + w * WINDOW
        start = pl.multiple_of(jnp.minimum(first, slots - WINDOW), 16)
        rel = row_ref[part] - start
        if not isinstance(w, int):
            rel = jnp.where(rel >= first - start, rel, -1)
        down = lax.broadcasted_iota(jnp.int32, (WINDOW, PART), 0)
        return pl.ds(start, WINDOW), (down == rel).astype(F32).astype(BF16)

    def place(part):
        return pl.ds(pl.multiple_of(part * PART, PART), PART)

    zone = slots * PART // trips

    def gather(step, carry):
        for j in range(parts):
            part = step * parts + j
            span, hot = window(part, 0)
            far2_ref[place(part), :] = dot_rows(hot, far_ref[span, :]).astype(BF16)
            blank = pl.ds(pl.multiple_of(part * zone, zone), zone)
            total_ref[blank, :] = jnp.zeros((zone, 2 * width), F32)

        @pl.when(most_ref[step] > 1)
        def _():
            for j in range(parts):
                part = step * parts + j

                def more(w, carry):
                    span, hot = window(part, w)
                    far2_ref[place(part), :] += dot_rows(hot, far_ref[span, :]).astype(BF16)
                    return carry

                lax.fori_loop(1, count_ref[part], more, 0)

        return carry

    def keeps(step):
        rows = pl.ds(pl.multiple_of(step * SUPER, SUPER), SUPER)
        return (
            pltpu.make_async_copy(inner_ref.at[rows], inner_hbm.at[rows], keep_sem.at[0, step]),
            pltpu.make_async_copy(dpre_ref.at[rows], dpre_hbm.at[rows], keep_sem.at[1, step]),
        )

    def mlp(step, carry):
        fetch(step).wait()
        chunks = SUPER // CHUNK
        state = [dict() for _ in range(chunks)]

        def here(c):
            return pl.ds(pl.multiple_of(step * SUPER + c * CHUNK, CHUNK), CHUNK)

        def stage0(c):
            v = state[c]
            a = own_ref[here(c), :width]
            b = far2_ref[here(c), :width]
            prod = (a.astype(F32) * b.astype(F32)).astype(BF16)
            v["x"] = jnp.concatenate([a, b, prod], axis=1)
            v["pre"] = dot(v["x"], w1_ref[...]) + bias_ref[...]
            ga = own_ref[here(c), width:]
            gb = far2_ref[here(c), width:]
            v["dm"] = (ga.astype(F32) + gb.astype(F32)).astype(BF16)
            v["dh"] = dot(v["dm"], w2t_ref[...])

        def stage1(c):
            v = state[c]
            pre = v.pop("pre")
            sig = 0.5 * jnp.tanh(0.5 * pre) + 0.5
            v["h"] = (pre * sig).astype(BF16)
            dpre = v.pop("dh") * (sig * (1.0 + pre * (1.0 - sig)))
            gbias_ref[...] += jnp.sum(dpre, axis=0, keepdims=True)
            v["dpre"] = dpre.astype(BF16)
            dpre_ref[here(c), :] = v["dpre"]

        def stage2(c):
            v = state[c]
            mb = dot(v["h"], w2_ref[...]).astype(BF16)
            inner_ref[here(c), :width] = mb
            outer_ref[here(c), :width] = mb
            v["dx"] = dot(v["dpre"], w1t_ref[...])
            rows1 = w1_ref.shape[0]
            grad_ref[:rows1, :] += dot_rows(v["x"], v["dpre"])
            grad_ref[rows1:, :] += dot_rows(v["dm"], v["h"])

        def stage3(c):
            v = state[c]
            dx = v.pop("dx")
            af = own_ref[here(c), :width].astype(F32)
            b = far2_ref[here(c), :width].astype(F32)
            dprod = dx[:, width:]
            inner_ref[here(c), width:] = (dprod * b).astype(BF16)
            outer_ref[here(c), width:] = (dx[:, :width] + dprod * af).astype(BF16)

        stages = [stage0, stage1, stage2, stage3]
        for t in range(chunks + len(stages) - 1):
            for s in ORDER:
                c = t - s
                if 0 <= c < chunks:
                    stages[s](c)
        for copy in keeps(step):
            copy.start()
        return carry

    def scatter(step, sent):
        for j in range(parts):
            part = step * parts + j
            span, hot = window(part, 0)
            total_ref[span, :] += dot(hot, outer_ref[place(part), :])

        @pl.when(most_ref[step] > 1)
        def _():
            for j in range(parts):
                part = step * parts + j

                def more(w, carry):
                    span, hot = window(part, w)
                    total_ref[span, :] += dot(hot, outer_ref[place(part), :])
                    return carry

                lax.fori_loop(1, count_ref[part], more, 0)

        steps = trips // BLOCK
        follow = base_ref[jnp.minimum((step + 1) * parts, steps * parts - 1)]
        ready = jnp.where(step == steps - 1, ndev // GROUP, follow // (GROUP * slots_per))
        lax.fori_loop(sent, ready, close, 0)
        return ready

    def leave(q):
        devices = pl.ds(q * GROUP, GROUP)
        return pltpu.make_async_copy(out_ref.at[devices], out_hbm.at[devices], out_sem.at[q])

    def close(q, carry):
        for i in range(GROUP):
            d = q * GROUP + i
            sums = total_ref[pl.ds(pl.multiple_of(d * slots_per, slots_per), slots_per), :]
            out_ref[d, :slots_per, :] = sums[:, :width].astype(BF16)
            out_ref[d, slots_per : 2 * slots_per, :] = sums[:, width:].astype(BF16)
        leave(q).start()
        return carry

    def close_grad(k, carry):
        for c in range(2):
            g = grad_ref[pl.ds(pl.multiple_of(k * 8, 8), 8), c * 128 : (c + 1) * 128]
            out_ref[2 * k + c, 2 * slots_per :, :] = g.astype(BF16)
        return carry

    lax.fori_loop(0, trips // BLOCK, gather, 0)
    lax.fori_loop(0, trips // SUPER, mlp, 0)
    lax.fori_loop(0, ndev // 2, close_grad, 0, unroll=4)
    lax.fori_loop(0, trips // BLOCK, scatter, 0)
    for q in range(ndev // GROUP):
        leave(q).wait()
    for step in range(trips // SUPER):
        for copy in keeps(step):
            copy.wait()


def triplets(remote, own, far, w1, bias, w2, ndev):
    trips = remote.shape[0]
    slots, pair = far.shape
    width = pair // 2
    hid = w1.shape[1]
    rows1 = w1.shape[0]
    steps = trips // BLOCK
    parts = BLOCK // PART
    blocks = remote.reshape(steps * parts, PART)
    base = jnp.minimum(blocks[:, 0] // 16 * 16, slots - WINDOW)
    count = (blocks[:, PART - 1] - base) // WINDOW + 1
    most = jnp.max(count.reshape(steps, parts), axis=1)
    row = remote.reshape(steps * parts, 1, PART)
    smem = pl.BlockSpec(memory_space=pltpu.SMEM)
    vmem = pl.BlockSpec(memory_space=pltpu.VMEM)
    hbm = pl.BlockSpec(memory_space=pltpu.HBM)
    return pl.pallas_call(
        triplet_kernel,
        in_specs=[smem] * 3 + [vmem, hbm] + [vmem] * 6,
        out_specs=[hbm, hbm, hbm, vmem],
        scratch_shapes=[
            pltpu.VMEM((slots, pair), F32),
            pltpu.VMEM((rows1 + width, hid), F32),
            pltpu.VMEM((trips, pair), BF16),
            pltpu.VMEM((trips, pair), BF16),
            pltpu.VMEM((trips, pair), BF16),
            pltpu.VMEM((trips, pair), BF16),
            pltpu.VMEM((trips, hid), BF16),
            pltpu.VMEM((ndev, 2 * slots // ndev + 8, width), BF16),
            pltpu.SemaphoreType.DMA((trips // SUPER,)),
            pltpu.SemaphoreType.DMA((2, trips // SUPER)),
            pltpu.SemaphoreType.DMA((ndev // GROUP,)),
        ],
        out_shape=[
            pltpu.HBM((trips, pair), BF16),
            pltpu.HBM((trips, hid), BF16),
            pltpu.HBM((ndev, 2 * slots // ndev + 8, width), BF16),
            jax.ShapeDtypeStruct((1, hid), F32),
        ],
        compiler_params=pltpu.CompilerParams(vmem_limit_bytes=36 * 2**20),
        cost_estimate=pl.CostEstimate(
            flops=2 * trips * 600000, bytes_accessed=20 * 2**20, transcendentals=trips * hid
        ),
        name="triplets",
    )(base, count, most, row, pltpu.with_memory_space_constraint(own, pltpu.HBM), far, w1, w1[width:].T, w2, w2.T, bias[None, :])


def pack_kernel(
    edges_hbm,
    cot_hbm,
    rows_hbm,
    count_hbm,
    table_hbm,
    out_hbm,
    rows_ref,
    count_ref,
    table_ref,
    index_ref,
    out_ref,
    in_sem,
    table_sem,
    out_sem,
):
    rows, width = edges_hbm.shape
    fetches = [
        pltpu.make_async_copy(rows_hbm, rows_ref, in_sem.at[0]),
        pltpu.make_async_copy(count_hbm, count_ref, in_sem.at[1]),
        pltpu.make_async_copy(edges_hbm, table_ref.at[:, pl.ds(0, width)], in_sem.at[2]),
        pltpu.make_async_copy(cot_hbm, table_ref.at[:, pl.ds(width, width)], in_sem.at[3]),
    ]
    for copy in fetches:
        copy.start()
    slots_per, ndev = rows_ref.shape
    block = out_ref.shape[1]
    group = block // slots_per
    fetches[0].wait()
    fetches[1].wait()
    slot = lax.broadcasted_iota(jnp.int32, (slots_per, ndev), 0)
    chosen = jnp.where(slot < count_ref[...], rows_ref[...], -1)
    for d in range(ndev):
        index_ref[d // group, (d % group) * slots_per : (d % group + 1) * slots_per, :] = (
            jnp.broadcast_to(chosen[:, d : d + 1], (slots_per, 128))
        )

    fetches[2].wait()
    fetches[3].wait()
    keep = pltpu.make_async_copy(table_ref, table_hbm, table_sem)
    keep.start()

    def send(g):
        start = pl.multiple_of(g * block, block)
        return pltpu.make_async_copy(out_ref.at[g], out_hbm.at[pl.ds(start, block)], out_sem.at[g])

    def body(g, carry):
        index = index_ref[g]
        lane = lax.broadcasted_iota(jnp.int32, index.shape, 1)
        total = None
        for k in range(0, rows, 256):
            hot = jnp.concatenate(
                [(index == lane + (k + c)).astype(F32).astype(BF16) for c in (0, 128)], axis=1
            )
            term = dot(hot, table_ref[k : k + 256, :])
            total = term if total is None else total + term
        out_ref[g] = total.astype(BF16)
        send(g).start()
        return carry

    groups = out_ref.shape[0]
    for g in range(groups):
        body(g, 0)
    for g in range(groups):
        send(g).wait()
    keep.wait()


def pack(edges, cotangent, rows_t, count):
    rows, width = edges.shape
    slots_per, ndev = rows_t.shape
    slots = slots_per * ndev
    groups = slots // PACK
    hbm = pl.BlockSpec(memory_space=pltpu.HBM)
    args = [pltpu.with_memory_space_constraint(v, pltpu.HBM) for v in (edges, cotangent, rows_t, count)]
    return pl.pallas_call(
        pack_kernel,
        in_specs=[hbm] * 4,
        out_specs=[hbm] * 2,
        out_shape=[
            pltpu.HBM((rows, 2 * width), BF16),
            pltpu.HBM((slots, 2 * width), BF16),
        ],
        scratch_shapes=[
            pltpu.VMEM((slots_per, ndev), jnp.int32),
            pltpu.VMEM((1, ndev), jnp.int32),
            pltpu.VMEM((rows, 2 * width), BF16),
            pltpu.VMEM((groups, PACK, 128), jnp.int32),
            pltpu.VMEM((groups, PACK, 2 * width), BF16),
            pltpu.SemaphoreType.DMA((4,)),
            pltpu.SemaphoreType.DMA,
            pltpu.SemaphoreType.DMA((groups,)),
        ],
        compiler_params=pltpu.CompilerParams(vmem_limit_bytes=36 * 2**20),
        cost_estimate=pl.CostEstimate(
            flops=4 * slots * rows * width, bytes_accessed=4 * 2**20, transcendentals=0
        ),
        name="pack",
    )(*args)


def unpack_kernel(shared_ref, first_ref, bias_ref, second_ref):
    width = shared_ref.shape[3]
    cut = first_ref.shape[0] // 8

    def piece(k, c):
        d = 2 * k + c
        return jnp.concatenate([shared_ref[d, 0], shared_ref[d, 1]], axis=0).astype(F32)

    for k in range(cut):
        for c in range(2):
            first_ref[8 * k : 8 * k + 8, c * width : (c + 1) * width] = piece(k, c)
    rest = shared_ref.shape[0] // 2 - cut
    for c in range(2):
        tall = jnp.concatenate([piece(cut + k, c) for k in range(rest)], axis=0)
        second_ref[c * width : (c + 1) * width, :] = tall.T
    ends = jnp.sum(shared_ref[:, 2].astype(F32), axis=0)
    for c in range(2):
        bias_ref[:, c * width : (c + 1) * width] = ends[c : c + 1, :] + ends[c + 2 : c + 3, :]


def unpack(shared, rows1, hid, width):
    vmem = pl.BlockSpec(memory_space=pltpu.VMEM)
    return pl.pallas_call(
        unpack_kernel,
        in_specs=[vmem],
        out_specs=[vmem] * 3,
        out_shape=[
            jax.ShapeDtypeStruct((rows1, hid), F32),
            jax.ShapeDtypeStruct((1, hid), F32),
            jax.ShapeDtypeStruct((hid, width), F32),
        ],
        cost_estimate=pl.CostEstimate(flops=0, bytes_accessed=2**20, transcendentals=0),
        name="unpack",
    )(pltpu.with_memory_space_constraint(shared, pltpu.VMEM))


def split(x):
    high = lax.reduce_precision(x, 8, 7)
    return high.astype(BF16), (x - high).astype(BF16)


def local(
    edges, cotangent, send_rows, send_count, trip_local, trip_remote, w_first, bias_first, w_second
):
    width = edges.shape[1]
    rows = edges.shape[0]
    ndev = lax.axis_size("phi") * lax.axis_size("eta")
    slots_per = send_rows.shape[2]
    slots = ndev * slots_per
    pair = 2 * width
    live = jnp.arange(slots_per, dtype=jnp.int32)[None, :] < send_count[0][:, None]
    chosen = jnp.where(live, send_rows[0], -1).reshape(slots)
    row_ids = jnp.arange(rows, dtype=jnp.int32)
    table, outgoing = pack(edges, cotangent, send_rows[0].T, send_count)
    outgoing = outgoing.reshape(ndev, slots_per, pair)
    arrived = lax.all_to_all(outgoing, AXES, split_axis=0, concat_axis=0, tiled=True)
    arrived = arrived.reshape(slots, pair)
    with jax.named_scope("order"):
        key = jnp.sort(trip_remote * rows + trip_local)
        remote = key // rows
        inner = key - remote * rows
    with jax.named_scope("own_rows"):
        own = dot((inner[:, None] == row_ids[None, :]).astype(BF16), table).astype(BF16)
    kept, dpre, outbound, gbias = triplets(
        remote, own, arrived, w_first, bias_first, w_second, ndev
    )
    returned = lax.all_to_all(outbound, AXES, split_axis=0, concat_axis=0, tiled=True)
    with jax.named_scope("own_sums"):
        d_inner = dot(dpre, w_first[:width].T) + kept[:, width:].astype(F32)
        inner_sums = jnp.concatenate([kept[:, :width], d_inner.astype(BF16)], axis=1)
        own_sum = dot((row_ids[:, None] == inner[None, :]).astype(BF16), inner_sums)
        own_sum = lax.optimization_barrier(table.astype(F32) + own_sum)
    hid = w_first.shape[1]
    mine = jnp.sum(returned[:, 2 * slots_per :, :].astype(F32), axis=0).astype(BF16)
    bias_high, bias_low = split(gbias)
    ends = jnp.concatenate([bias_high, bias_low], axis=0).reshape(1, 4, width)
    share = jnp.concatenate([mine.reshape(2, 4, width), ends], axis=0)
    share = jnp.broadcast_to(share[None], (ndev,) + share.shape)
    shared = lax.all_to_all(share, AXES, split_axis=0, concat_axis=0, tiled=True)
    with jax.named_scope("far_sums"):
        back = jnp.concatenate(
            [returned[:, :slots_per, :], returned[:, slots_per : 2 * slots_per, :]], axis=2
        ).reshape(slots, pair)
        far_sum = dot((row_ids[:, None] == chosen[None, :]).astype(BF16), back)
    both = (own_sum + far_sum).astype(BF16)
    grad_first, grad_bias, grad_second = unpack(shared, w_first.shape[0], hid, width)
    return (both[:, :width], both[:, width:], grad_first, grad_bias.reshape(hid), grad_second)


def solution(mesh):
    in_specs = (
        P(AXES, None),
        P(AXES, None),
        P(AXES, None, None),
        P(AXES, None),
        P(AXES),
        P(AXES),
        P(),
        P(),
        P(),
    )
    out_specs = (P(AXES, None), P(AXES, None), P(), P(), P())
    return jax.shard_map(local, mesh=mesh, in_specs=in_specs, out_specs=out_specs, check_vma=False)
```
